256 devices in a mesh: gy: 32 (over z, x), gz: 8 (over y, core).
Axes of the slice: x: 4, y: 4, z: 8, core: 2. Of those that a mesh axis runs over, the one named last changes fastest.
Arguments:
- heat_scalar_window: float32 [512, 64, 2048], P('gy', 'gz'), may hold values from -6 to 6
- flow_speed_vector: bfloat16 [3, 512, 64, 2048], P(None, 'gy', 'gz'), may hold values from -4 to 4
Outputs:
- updated: float32 [512, 64, 2048], P('gy', 'gz')
The draws below stay inside these ranges and needn't reach their ends.
All inputs are finite; a program needn't handle non-finite values.
Results may differ from the reference program's by a relative error of at most 0.0003.
Values sent between devices are 32-bit elements; how exact they have to be, the bound alone decides.
No kernel may reach another device: no remote copies, remote signals or barrier semaphores. Data moves between devices by JAX's collectives and lax.ppermute only.
A program may use at most 64 MiB of HBM per device.

```python
import jax
import jax.numpy as jnp
from jax import lax

GRID_SPAN_EAST = 2048
RX = 1
RY = 768
RZ = 192
GRID_SPAN_NORTH = 512
GRID_SPAN_VERTICAL = 64


def block_levels(key, shape, split, smallest, high):
    factor_of = 1.0
    for position, parts in split:
        draws = jax.random.uniform(jax.random.fold_in(jax.random.fold_in(key, 6), position), (parts,), jnp.float32, smallest / len(split), high / len(split))
        factor_of = factor_of * jnp.repeat(jnp.exp(draws), shape[position] // parts).reshape((-1,) + (1,) * (len(shape) - 1 - position))
    return factor_of


def noise(own_key, extent, scale, reach, split=(), kind=jnp.bfloat16):
    entries = jax.random.normal(own_key, extent, jnp.float32) * scale
    if len(split) > 0:
        entries = block_levels(own_key, extent, split, -0.22, 0.18) * entries
    return jnp.clip(entries, min=-reach, max=reach).astype(kind)


def setup_inputs(seed: int = 0) -> dict:
    key_of = jax.random.split(jax.random.key(seed), 3)
    return {
        "heat_scalar_window": noise(key_of[0], (GRID_SPAN_NORTH, GRID_SPAN_VERTICAL, GRID_SPAN_EAST), 1.0, 6.0, ((0, 32), (1, 8)), jnp.float32),
        "flow_speed_vector": noise(key_of[1], (3, GRID_SPAN_NORTH, GRID_SPAN_VERTICAL, GRID_SPAN_EAST), 1.0, 4.0, ((1, 32), (2, 8))),
    }


EXACT = lax.Precision.HIGHEST
thermal_conduction_coefficient = 0.15

def line_inverse(line_count, ratio_value):
    coupling = jnp.float32(ratio_value)
    half_step = 0.5 / coupling
    decay_base = 1.0 + half_step - jnp.sqrt(half_step * (2.0 + half_step))
    places = jnp.arange(line_count, dtype=jnp.float32)
    small_index = jnp.minimum(places[:, None], places[None, :])
    large_index = jnp.maximum(places[:, None], places[None, :])
    span_value = jnp.float32(line_count)
    numer = decay_base ** (large_index - small_index + 1.0) * (1.0 - decay_base ** (2.0 * (small_index + 1.0))) * (1.0 - decay_base ** (2.0 * (span_value - large_index)))
    denom = coupling * (1.0 - decay_base * decay_base) * (1.0 - decay_base ** (2.0 * span_value + 2.0))
    return numer / denom

def known_contribution(heat_scalar_window, flow_speed_vector):
    haloed_array = jnp.pad(heat_scalar_window, 1)
    northern_adjacent = haloed_array[2:, 1:-1, 1:-1]
    southern_adjacent = haloed_array[:-2, 1:-1, 1:-1]
    ceiling_adjacent = haloed_array[1:-1, 2:, 1:-1]
    bottom_adjacent = haloed_array[1:-1, :-2, 1:-1]
    eastern_adjacent = haloed_array[1:-1, 1:-1, 2:]
    western_adjacent = haloed_array[1:-1, 1:-1, :-2]
    laplacian_contribution = eastern_adjacent + western_adjacent + northern_adjacent + southern_adjacent + ceiling_adjacent + bottom_adjacent - 6.0 * heat_scalar_window
    retained_remainder = flow_speed_vector[0].astype(jnp.float32) * (eastern_adjacent - western_adjacent) + flow_speed_vector[1].astype(jnp.float32) * (northern_adjacent - southern_adjacent) + flow_speed_vector[2].astype(jnp.float32) * (ceiling_adjacent - bottom_adjacent)
    return heat_scalar_window + thermal_conduction_coefficient * laplacian_contribution - 0.5 * retained_remainder

def reference(heat_scalar_window, flow_speed_vector):
    forcing_contribution = known_contribution(heat_scalar_window, flow_speed_vector)
    inverse_x = line_inverse(GRID_SPAN_EAST, RX)
    inverse_y = line_inverse(GRID_SPAN_NORTH, RY)
    inverse_z = line_inverse(GRID_SPAN_VERTICAL, RZ)
    along_x = jnp.dot(forcing_contribution, inverse_x, precision=EXACT)
    along_y = jnp.einsum('ab,bzx->azx', inverse_y, along_x, precision=EXACT)
    return jnp.einsum('ab,ybx->yax', inverse_z, along_y, precision=EXACT)
```

```python
import jax
import jax.numpy as jnp
import numpy as np
from jax import lax
from jax.experimental import pallas as pl
from jax.experimental.pallas import tpu as pltpu
from jax.sharding import PartitionSpec as P

NX, NY, NZ = 2048, 512, 64
RX, RY, RZ = 1, 768, 192
DY, DZ = 32, 8
LY, LZ = NY // DY, NZ // DZ
XB = 256
NB = NX // XB
KAPPA = 0.15
F32, BF16 = jnp.float32, jnp.bfloat16


def decay(ratio):
    half = 0.5 / ratio
    return 1.0 + half - np.sqrt(half * (2.0 + half))


def line_factors(count, ratio):
    q = decay(ratio)
    i = np.arange(count)
    low = 1.0 - q ** (2.0 * (i + 1))
    high = 1.0 - q ** (2.0 * (count - i))
    denom = ratio * (1.0 - q * q) * (1.0 - q ** (2.0 * count + 2))
    return q, low, high, denom


def split_line(count, ratio, parts):
    q, low, high, denom = line_factors(count, ratio)
    size = count // parts
    low, high = low.reshape(parts, size), high.reshape(parts, size)
    m = np.arange(size)
    small = np.minimum(m[:, None], m[None])
    large = np.maximum(m[:, None], m[None])
    block = q ** (large - small + 1.0) * low[:, small] * high[:, large] / denom
    up = q ** (size - 1.0 - m) * low
    down = q ** (1.0 * m) * high
    from_low = q ** (m + 2.0) * high / denom
    from_high = q ** (size + 1.0 - m) * low / denom
    return block, up, down, from_low, from_high, q**size


def tables():
    block_y, up_y, down_y, gl_y, gh_y, step_y = split_line(NY, RY, DY)
    block_z, up_z, down_z, gl_z, gh_z, step_z = split_line(NZ, RZ, DZ)
    ty = np.zeros((DY, 24, 128))
    ty[:, :LY] = np.repeat(block_y, LZ, axis=2)
    ty[:, LY] = np.repeat(up_y, LZ, axis=1)
    ty[:, LY + 1] = np.repeat(down_y, LZ, axis=1)
    tz = np.zeros((DZ, 24, 128))
    tz[:, :LZ] = np.tile(block_z, (1, 1, LY))
    tz[:, LZ : 2 * LZ] = np.tile(np.eye(LZ), (1, LY))[None]
    tz[:, 16] = np.tile(up_z, (1, LY))
    tz[:, 17] = np.tile(down_z, (1, LY))
    tm = np.zeros((DZ, 16, 128))
    tm[:, :8, :8] = block_z
    for e in range(DZ):
        for p in range(DZ):
            if p > e:
                tm[e, 8 + p, :8] = up_z[e] * step_z ** (p - e - 1)
            if p < e:
                tm[e, 8 + p, :8] = down_z[e] * step_z ** (e - p - 1)
    tm[:, :8, 8] = gl_z
    tm[:, :8, 9] = gh_z
    tg = np.zeros((DY, 16, 128))
    tg[:, :, 0] = gl_y
    tg[:, :, 1] = gh_y
    sy = np.zeros((DY, 128))
    sy[:, :16] = gl_y
    sy[:, 16:32] = gh_y
    sz = np.zeros((DZ, 128))
    for e in range(DZ):
        for p in range(DZ):
            if p < e:
                sz[e, p] = step_z ** (e - p - 1)
            if p > e:
                sz[e, 8 + p] = step_z ** (p - e - 1)
    f32 = lambda a: a.astype(np.float32)
    return f32(ty), f32(tz), f32(tm), f32(tg), f32(sy), f32(sz), float(step_y)


TY, TZ, TM, TG, SY, SZ, STEP_Y = tables()
QX = decay(RX)


def x_weights():
    c = np.arange(XB)
    w = (QX ** (np.abs(c[:, None] - c[None]) + 1.0) / (RX * (1 - QX * QX))).astype(np.float32)
    high = w.astype(jnp.bfloat16)
    low = (w - high.astype(np.float32)).astype(jnp.bfloat16)
    edge = np.zeros((8, 128), np.float32)
    edge[0] = QX ** (np.arange(128) + 1.0)
    edge[1] = QX ** (128.0 - np.arange(128))
    return np.stack([high, low]), edge


WX, EDGE = x_weights()


def halves(value):
    high = value.astype(BF16)
    return high, (value - high.astype(F32)).astype(BF16)


def mm(a, b):
    return jnp.dot(a, b, preferred_element_type=F32)


def local_kernel(t_ref, v_ref, y1_ref, y2_ref, z1_ref, z2_ref, ty_ref, tz_ref, wx_ref, edge_ref,
                 loc_ref, a_ref, c_ref, fh, fl, g, ghl):
    d, e = lax.axis_index("gy"), lax.axis_index("gz")
    odd_y, odd_z = (d % 2) == 1, (e % 2) == 1
    zi = lax.broadcasted_iota(jnp.int32, (LZ, NX), 0)
    xi = lax.broadcasted_iota(jnp.int32, (LZ, NX), 1)
    north_halo = jnp.where(odd_y, y2_ref[...], y1_ref[...])
    south_halo = jnp.where(odd_y, y1_ref[...], y2_ref[...])
    for y in range(LY):
        t = t_ref[y]
        north = t_ref[y + 1] if y < LY - 1 else north_halo
        south = t_ref[y - 1] if y > 0 else south_halo
        h1, h2 = z1_ref[y : y + 1, :], z2_ref[y : y + 1, :]
        above = jnp.where(odd_z, h2, h1)
        below = jnp.where(odd_z, h1, h2)
        ceil = jnp.where(zi == LZ - 1, above, pltpu.roll(t, LZ - 1, 0))
        floor = jnp.where(zi == 0, below, pltpu.roll(t, 1, 0))
        east = jnp.where(xi == NX - 1, 0.0, pltpu.roll(t, NX - 1, 1))
        west = jnp.where(xi == 0, 0.0, pltpu.roll(t, 1, 1))
        lap = ((east + west) + (north + south)) + (ceil + floor) - 6.0 * t
        adv = (v_ref[0, y].astype(F32) * (east - west) + v_ref[1, y].astype(F32) * (north - south)
               + v_ref[2, y].astype(F32) * (ceil - floor))
        f = t + KAPPA * lap - 0.5 * adv
        high, low = f.astype(BF16).astype(F32), None
        for b in range(NB):
            part = f[:, b * XB : (b + 1) * XB]
            g[b, y * LZ : (y + 1) * LZ, :] = part
    for b in range(NB):
        high, low = halves(g[b])
        fh[b] = high
        fl[b] = low
    wh, wl = wx_ref[0], wx_ref[1]
    rows = LY * LZ
    xh = fh[...].reshape(NB * rows, XB)
    xl = fl[...].reshape(NB * rows, XB)
    g[...] = (mm(xh, wh) + (mm(xh, wl) + mm(xl, wh))).reshape(NB, rows, XB)
    left, right = edge_ref[0:1, :], edge_ref[1:2, :]
    for b in range(NB):
        before = g[b - 1, :, XB - 1 :] if b > 0 else g[0, :, :1] * (-QX)
        after = g[b + 1, :, :1] if b < NB - 1 else g[NB - 1, :, XB - 1 :] * (-QX)
        lo = g[b, :, :128] + before * left
        hi = g[b, :, 128:] + after * right
        for k, part in ((0, lo), (1, hi)):
            high, low = halves(part)
            at = b * XB + k * 128
            ghl[:rows, at : at + 128] = high
            ghl[rows:, at : at + 128] = low
    my = ty_ref[d]
    mz = tz_ref[e]
    own = (my[:LY][:, None, :] * mz[:LZ][None]).reshape(rows, 128)
    a_rows = jnp.concatenate([my[LY : LY + 1] * mz[8:16], my[LY + 1 : LY + 2] * mz[8:16]], axis=0)
    c_rows = jnp.concatenate([my[:LY] * mz[16:17], my[:LY] * mz[17:18]], axis=0)
    m = jnp.concatenate([own, a_rows, c_rows], axis=0)
    mh, ml = halves(m)
    first = jnp.concatenate([mh, mh], axis=1)
    for b in range(NB):
        cols = slice(b * XB, (b + 1) * XB)
        out = mm(first, ghl[:, cols]) + mm(ml, ghl[:rows, cols])
        loc_ref[:, :, cols] = out[:rows].reshape(LY, LZ, XB)
        c_ref[0, :, cols] = out[rows + 16 : rows + 32]
        c_ref[1, :, cols] = out[rows + 32 :]
        for k in range(2):
            for h in range(2):
                t = b * 2 + h
                tile = out[rows + 8 * k : rows + 8 * k + 8, h * 128 : (h + 1) * 128]
                a_ref[pl.ds((t // 4) * 8 + k * 4 + t % 4, 8, stride=32), :] = tile


def scan_kernel(r_ref, o_ref):
    low_half = lax.broadcasted_iota(jnp.int32, (8, 128), 0) < 4
    state = jnp.zeros((8, 128), F32)
    ahead = []
    for d in range(DY):
        ahead.append(state)
        state = state * STEP_Y + r_ref[d]
    state = jnp.zeros((8, 128), F32)
    for d in range(DY - 1, -1, -1):
        o_ref[d] = jnp.where(low_half, ahead[d], state)
        state = state * STEP_Y + r_ref[d]


def mixed_kernel(p_ref, tm_ref, dz_ref, s_ref):
    e = lax.axis_index("gz")
    tm = tm_ref[e]
    own = [jnp.broadcast_to(tm[:8, w : w + 1], (8, 128)) for w in range(8)]
    out = [jnp.broadcast_to(tm[8:, w : w + 1], (8, 128)) for w in range(8)]
    for k in range(2):
        for t in range(16):
            p = p_ref[pl.ds((t // 4) * 8 + k * 4 + t % 4, 8, stride=32), :]
            one = own[0] * p[0:1]
            two = out[0] * p[0:1]
            for w in range(1, 8):
                one += own[w] * p[w : w + 1]
                two += out[w] * p[w : w + 1]
            dz_ref[k, :, t * 128 : (t + 1) * 128] = one
            s_ref[pl.ds(k * 16 + t, 8, stride=32), :] = two


CH = 512


def final_kernel(loc_ref, dz_ref, cg_ref, r_ref, tm_ref, tg_ref, sy_ref, sz_ref, o_ref, cl, ch):
    d, e = lax.axis_index("gy"), lax.axis_index("gz")
    j = pl.program_id(0)
    tg = tg_ref[d]
    ga = jnp.broadcast_to(tg[:, 0:1], (16, 128))
    gb = jnp.broadcast_to(tg[:, 1:2], (16, 128))
    for i in range(CH // 128):
        cols = slice(i * 128, (i + 1) * 128)
        t = j * (CH // 128) + i
        low = jnp.zeros((16, 128), F32)
        high = jnp.zeros((16, 128), F32)
        for p in range(DZ):
            low += sz_ref[e, p] * cg_ref[p, 0, :, cols]
            high += sz_ref[e, 8 + p] * cg_ref[p, 1, :, cols]
        rows = []
        for k in range(2):
            lo = jnp.zeros((1, 128), F32)
            hi = jnp.zeros((1, 128), F32)
            for p in range(DZ):
                row = r_ref[pl.ds(p * 32 + k * 16 + t, 1), :]
                lo += jnp.where(p < e, row, 0.0)
                hi += jnp.where(p > e, row, 0.0)
            rows.append((lo, hi))
        cl[:, cols] = low + ga * rows[0][0] + gb * rows[1][0]
        ch[:, cols] = high + ga * rows[0][1] + gb * rows[1][1]
    tm = tm_ref[e]
    hl = jnp.broadcast_to(tm[:8, 8:9], (8, CH))
    hh = jnp.broadcast_to(tm[:8, 9:10], (8, CH))
    for l in range(LY):
        o_ref[l] = (loc_ref[l] + sy_ref[d, l] * dz_ref[0] + sy_ref[d, 16 + l] * dz_ref[1]
                    + (hl * cl[l : l + 1, :] + hh * ch[l : l + 1, :]))


VMEM = pl.BlockSpec(memory_space=pltpu.VMEM)
SMEM = pl.BlockSpec(memory_space=pltpu.SMEM)


def params(mib):
    return pltpu.CompilerParams(vmem_limit_bytes=mib * 2**20)


def pairs(count, odd):
    out = []
    for i in range(count):
        j = i + 1 if (i % 2 == 1) == odd else i - 1
        if 0 <= j < count:
            out.append((i, j))
    return out


def on_device(temp, vel):
    d, e = lax.axis_index("gy"), lax.axis_index("gz")
    odd_y, odd_z = d % 2, e % 2
    face_y = lambda last: lax.dynamic_slice_in_dim(temp, last * (LY - 1), 1, 0)[0]
    face_z = lambda last: jnp.where(last == 1, temp[:, LZ - 1], temp[:, 0])
    y1 = lax.ppermute(face_y(1 - odd_y), "gy", pairs(DY, False))
    y2 = lax.ppermute(face_y(odd_y), "gy", pairs(DY, True))
    z1 = lax.ppermute(face_z(1 - odd_z), "gz", pairs(DZ, False))
    z2 = lax.ppermute(face_z(odd_z), "gz", pairs(DZ, True))
    rows = LY * LZ
    loc, a, c = pl.pallas_call(
        local_kernel,
        out_shape=(
            jax.ShapeDtypeStruct((LY, LZ, NX), F32),
            jax.ShapeDtypeStruct((256, 128), F32),
            jax.ShapeDtypeStruct((2, LY, NX), F32),
        ),
        in_specs=[VMEM] * 10,
        out_specs=(VMEM, VMEM, VMEM),
        scratch_shapes=[
            pltpu.VMEM((NB, rows, XB), BF16),
            pltpu.VMEM((NB, rows, XB), BF16),
            pltpu.VMEM((NB, rows, XB), F32),
            pltpu.VMEM((2 * rows, NX), BF16),
        ],
        compiler_params=params(40),
        name="local",
    )(temp, vel, y1, y2, z1, z2, TY, TZ, WX, EDGE)
    cg = lax.all_gather(c, "gz")
    r1 = lax.all_to_all(a.reshape(DY, 8, 128), "gy", 0, 0)
    scanned = pl.pallas_call(
        scan_kernel,
        out_shape=jax.ShapeDtypeStruct((DY, 8, 128), F32),
        in_specs=[VMEM],
        out_specs=VMEM,
        name="scan",
    )(r1)
    r2 = lax.all_to_all(scanned, "gy", 0, 0)
    dz, s = pl.pallas_call(
        mixed_kernel,
        out_shape=(
            jax.ShapeDtypeStruct((2, LZ, NX), F32),
            jax.ShapeDtypeStruct((256, 128), F32),
        ),
        in_specs=[VMEM] * 2,
        out_specs=(VMEM, VMEM),
        name="mixed",
    )(r2.reshape(256, 128), TM)
    r3 = lax.all_to_all(s.reshape(DZ, 32, 128), "gz", 0, 0)
    return pl.pallas_call(
        final_kernel,
        grid=(NX // CH,),
        out_shape=jax.ShapeDtypeStruct((LY, LZ, NX), F32),
        in_specs=[
            pl.BlockSpec((LY, LZ, CH), lambda j: (0, 0, j)),
            pl.BlockSpec((2, LZ, CH), lambda j: (0, 0, j)),
            pl.BlockSpec((DZ, 2, LY, CH), lambda j: (0, 0, 0, j)),
            VMEM, VMEM, VMEM, SMEM, SMEM,
        ],
        out_specs=pl.BlockSpec((LY, LZ, CH), lambda j: (0, 0, j)),
        scratch_shapes=[pltpu.VMEM((LY, CH), F32)] * 2,
        compiler_params=params(24),
        name="final",
    )(loc, dz, cg, r3.reshape(256, 128), TM, TG, SY, SZ)


def solution(mesh):
    return jax.shard_map(
        on_device,
        mesh=mesh,
        in_specs=(P("gy", "gz", None), P(None, "gy", "gz", None)),
        out_specs=P("gy", "gz", None),
        check_vma=False,
    )
```

```python
import jax
import jax.numpy as jnp
import numpy as np
from jax import lax
from jax.experimental import pallas as pl
from jax.experimental.pallas import tpu as pltpu
from jax.sharding import PartitionSpec as P

NX, NY, NZ = 2048, 512, 64
RX, RY, RZ = 1, 768, 192
DY, DZ = 32, 8
LY, LZ = NY // DY, NZ // DZ
XB = 256
NB = NX // XB
KAPPA = 0.15
F32, BF16 = jnp.float32, jnp.bfloat16


def decay(ratio):
    half = 0.5 / ratio
    return 1.0 + half - np.sqrt(half * (2.0 + half))


def line_factors(count, ratio):
    q = decay(ratio)
    i = np.arange(count)
    low = 1.0 - q ** (2.0 * (i + 1))
    high = 1.0 - q ** (2.0 * (count - i))
    denom = ratio * (1.0 - q * q) * (1.0 - q ** (2.0 * count + 2))
    return q, low, high, denom


def split_line(count, ratio, parts):
    q, low, high, denom = line_factors(count, ratio)
    size = count // parts
    low, high = low.reshape(parts, size), high.reshape(parts, size)
    m = np.arange(size)
    small = np.minimum(m[:, None], m[None])
    large = np.maximum(m[:, None], m[None])
    block = q ** (large - small + 1.0) * low[:, small] * high[:, large] / denom
    up = q ** (size - 1.0 - m) * low
    down = q ** (1.0 * m) * high
    from_low = q ** (m + 2.0) * high / denom
    from_high = q ** (size + 1.0 - m) * low / denom
    return block, up, down, from_low, from_high, q**size


def tables():
    block_y, up_y, down_y, gl_y, gh_y, step_y = split_line(NY, RY, DY)
    block_z, up_z, down_z, gl_z, gh_z, step_z = split_line(NZ, RZ, DZ)
    lines = np.zeros((DY + DZ, 24, 128))
    ty, tz = lines[:DY], lines[DY:]
    ty[:, :LY] = np.repeat(block_y, LZ, axis=2)
    ty[:, LY] = np.repeat(up_y, LZ, axis=1)
    ty[:, LY + 1] = np.repeat(down_y, LZ, axis=1)
    tz[:, :LZ] = np.tile(block_z, (1, 1, LY))
    tz[:, LZ : 2 * LZ] = np.tile(np.eye(LZ), (1, LY))[None]
    tz[:, 16] = np.tile(up_z, (1, LY))
    tz[:, 17] = np.tile(down_z, (1, LY))
    tz[:, 18] = QX ** (np.arange(128) + 1.0)
    tz[:, 19] = QX ** (128.0 - np.arange(128))
    sums = np.zeros((DY + DZ, 16, 128))
    tm = sums[DY:]
    tm[:, :8, :8] = block_z
    for e in range(DZ):
        for p in range(DZ):
            if p > e:
                tm[e, 8 + p, :8] = up_z[e] * step_z ** (p - e - 1)
            if p < e:
                tm[e, 8 + p, :8] = down_z[e] * step_z ** (e - p - 1)
    tm[:, :8, 8] = gl_z
    tm[:, :8, 9] = gh_z
    sums[:DY, :, 0] = gl_y
    sums[:DY, :, 1] = gh_y
    scal = np.zeros((DY, 128))
    scal[:, :16] = gl_y
    scal[:, 16:32] = gh_y
    f32 = lambda a: a.astype(np.float32)
    return f32(lines), f32(sums), f32(scal), float(step_y), float(step_z)


QX = decay(RX)
LINES, SUMS, SCAL, STEP_Y, STEP_Z = tables()


def x_weights():
    c = np.arange(XB)
    w = (QX ** (np.abs(c[:, None] - c[None]) + 1.0) / (RX * (1 - QX * QX))).astype(np.float32)
    high = w.astype(jnp.bfloat16)
    low = (w - high.astype(np.float32)).astype(jnp.bfloat16)
    return np.stack([high, low])


WX = x_weights()


def halves(value):
    high = value.astype(BF16)
    return high, (value - high.astype(F32)).astype(BF16)


def mm(a, b):
    return jnp.dot(a, b, preferred_element_type=F32)


def start(*pairs_and_sem):
    copies = [pltpu.make_async_copy(*p) for p in pairs_and_sem]
    for c in copies:
        c.start()
    return copies


def faces_kernel(t_hbm, t_ref, y1_ref, y2_ref, z1_ref, z2_ref, sem):
    d, e = lax.axis_index("gy"), lax.axis_index("gz")
    odd_y, odd_z = (d % 2) == 1, (e % 2) == 1
    load = pltpu.make_async_copy(t_hbm, t_ref, sem)
    load.start()
    load.wait()
    first, last = t_ref[0], t_ref[LY - 1]
    y1_ref[...] = jnp.where(odd_y, first, last)
    y2_ref[...] = jnp.where(odd_y, last, first)
    for y in range(LY):
        bottom, top = t_ref[y, 0:1, :], t_ref[y, LZ - 1 : LZ, :]
        z1_ref[y : y + 1, :] = jnp.where(odd_z, bottom, top)
        z2_ref[y : y + 1, :] = jnp.where(odd_z, top, bottom)


def local_kernel(t_ref, v_hbm, y1_ref, y2_ref, z1_ref, z2_ref, lines_hbm, wx_hbm,
                 loc_ref, a_ref, c_ref, fh, fl, g, ghl, v_ref, ty_ref, tz_ref, wx_ref, sems):
    d, e = lax.axis_index("gy"), lax.axis_index("gz")
    loads = start((v_hbm, v_ref, sems.at[0]), (wx_hbm, wx_ref, sems.at[1]),
                  (lines_hbm.at[d], ty_ref, sems.at[2]), (lines_hbm.at[DY + e], tz_ref, sems.at[3]))
    odd_y, odd_z = (d % 2) == 1, (e % 2) == 1
    zi = lax.broadcasted_iota(jnp.int32, (LZ, NX), 0)
    xi = lax.broadcasted_iota(jnp.int32, (LZ, NX), 1)
    north_halo = jnp.where(odd_y, y2_ref[...], y1_ref[...])
    south_halo = jnp.where(odd_y, y1_ref[...], y2_ref[...])
    loads[0].wait()
    for y in range(LY):
        t = t_ref[y]
        north = t_ref[y + 1] if y < LY - 1 else north_halo
        south = t_ref[y - 1] if y > 0 else south_halo
        h1, h2 = z1_ref[y : y + 1, :], z2_ref[y : y + 1, :]
        above = jnp.where(odd_z, h2, h1)
        below = jnp.where(odd_z, h1, h2)
        ceil = jnp.where(zi == LZ - 1, above, pltpu.roll(t, LZ - 1, 0))
        floor = jnp.where(zi == 0, below, pltpu.roll(t, 1, 0))
        east = jnp.where(xi == NX - 1, 0.0, pltpu.roll(t, NX - 1, 1))
        west = jnp.where(xi == 0, 0.0, pltpu.roll(t, 1, 1))
        lap = ((east + west) + (north + south)) + (ceil + floor) - 6.0 * t
        adv = (v_ref[0, y].astype(F32) * (east - west) + v_ref[1, y].astype(F32) * (north - south)
               + v_ref[2, y].astype(F32) * (ceil - floor))
        f = t + KAPPA * lap - 0.5 * adv
        for b in range(NB):
            part = f[:, b * XB : (b + 1) * XB]
            g[b, y * LZ : (y + 1) * LZ, :] = part
    for b in range(NB):
        high, low = halves(g[b])
        fh[b] = high
        fl[b] = low
    for load in loads[1:]:
        load.wait()
    wh, wl = wx_ref[0], wx_ref[1]
    rows = LY * LZ
    xh = fh[...].reshape(NB * rows, XB)
    xl = fl[...].reshape(NB * rows, XB)
    g[...] = (mm(xh, wh) + (mm(xh, wl) + mm(xl, wh))).reshape(NB, rows, XB)
    left, right = tz_ref[18:19, :], tz_ref[19:20, :]
    for b in range(NB):
        before = g[b - 1, :, XB - 1 :] if b > 0 else g[0, :, :1] * (-QX)
        after = g[b + 1, :, :1] if b < NB - 1 else g[NB - 1, :, XB - 1 :] * (-QX)
        lo = g[b, :, :128] + before * left
        hi = g[b, :, 128:] + after * right
        for k, part in ((0, lo), (1, hi)):
            high, low = halves(part)
            at = b * XB + k * 128
            ghl[:rows, at : at + 128] = high
            ghl[rows:, at : at + 128] = low
    my = ty_ref[...]
    mz = tz_ref[...]
    own = (my[:LY][:, None, :] * mz[:LZ][None]).reshape(rows, 128)
    a_rows = jnp.concatenate([my[LY : LY + 1] * mz[8:16], my[LY + 1 : LY + 2] * mz[8:16]], axis=0)
    c_rows = jnp.concatenate([my[:LY] * mz[16:17], my[:LY] * mz[17:18]], axis=0)
    m = jnp.concatenate([own, a_rows, c_rows], axis=0)
    mh, ml = halves(m)
    first = jnp.concatenate([mh, mh], axis=1)
    for b in range(NB):
        cols = slice(b * XB, (b + 1) * XB)
        out = mm(first, ghl[:, cols]) + mm(ml, ghl[:rows, cols])
        loc_ref[:, :, cols] = out[:rows].reshape(LY, LZ, XB)
        c_ref[0, :, cols] = out[rows + 16 : rows + 32]
        c_ref[1, :, cols] = out[rows + 32 :]
        for k in range(2):
            for h in range(2):
                t = b * 2 + h
                tile = out[rows + 8 * k : rows + 8 * k + 8, h * 128 : (h + 1) * 128]
                a_ref[pl.ds((t // 4) * 8 + k * 4 + t % 4, 8, stride=32), :] = tile


def scan_kernel(r_ref, c_ref, x_ref, o_ref, tot_ref, pre_ref):
    low_half = lax.broadcasted_iota(jnp.int32, (8, 128), 0) < 4
    state = jnp.zeros((8, 128), F32)
    ahead = []
    for d in range(DY):
        ahead.append(state)
        state = state * STEP_Y + r_ref[d]
    state = jnp.zeros((8, 128), F32)
    for d in range(DY - 1, -1, -1):
        o_ref[d] = jnp.where(low_half, ahead[d], state)
        state = state * STEP_Y + r_ref[d]
    e = lax.axis_index("gz")
    upper = (e % 2) == 1
    near, far = jnp.where(upper, 1.0, STEP_Z), jnp.where(upper, STEP_Z, 1.0)
    tot_ref[0] = near * c_ref[0] + far * x_ref[0]
    tot_ref[1] = far * c_ref[1] + near * x_ref[1]
    pre_ref[0] = jnp.where(upper, x_ref[0], 0.0)
    pre_ref[1] = jnp.where(upper, 0.0, x_ref[1])


def mixed_kernel(p_ref, tot_ref, x_ref, pre_ref, sums_hbm, dz_ref, s_ref, send_ref, pre2_ref, tm_ref, sem):
    e = lax.axis_index("gz")
    load = pltpu.make_async_copy(sums_hbm.at[DY + e], tm_ref, sem)
    load.start()
    upper = ((e // 2) % 2) == 1
    odd = (e % 2) == 1
    two = STEP_Z * STEP_Z
    near, far = jnp.where(upper, 1.0, two), jnp.where(upper, two, 1.0)
    top = (e // 4) == 1
    send_ref[...] = jnp.where(top, far * tot_ref[1] + near * x_ref[1], near * tot_ref[0] + far * x_ref[0])
    low = jnp.where(odd, STEP_Z, 1.0)
    high = jnp.where(odd, 1.0, STEP_Z)
    pre2_ref[0] = pre_ref[0] + jnp.where(upper, low * x_ref[0], 0.0)
    pre2_ref[1] = pre_ref[1] + jnp.where(upper, 0.0, high * x_ref[1])
    load.wait()
    tm = tm_ref[...]
    own = [jnp.broadcast_to(tm[:8, w : w + 1], (8, 128)) for w in range(8)]
    out = [jnp.broadcast_to(tm[8:, w : w + 1], (8, 128)) for w in range(8)]
    for k in range(2):
        for t in range(16):
            p = p_ref[pl.ds((t // 4) * 8 + k * 4 + t % 4, 8, stride=32), :]
            one = own[0] * p[0:1]
            two = out[0] * p[0:1]
            for w in range(1, 8):
                one += own[w] * p[w : w + 1]
                two += out[w] * p[w : w + 1]
            dz_ref[k, :, t * 128 : (t + 1) * 128] = one
            s_ref[pl.ds(k * 16 + t, 8, stride=32), :] = two


def final_kernel(loc_ref, dz_ref, pre_ref, x_ref, r_ref, sums_hbm, scal_ref, o_hbm,
                 cl, ch, o_ref, tg_ref, tm_ref, sems):
    d, e = lax.axis_index("gy"), lax.axis_index("gz")
    loads = start((sums_hbm.at[d], tg_ref, sems.at[0]), (sums_hbm.at[DY + e], tm_ref, sems.at[1]))
    lo = jnp.zeros((32, 128), F32)
    hi = jnp.zeros((32, 128), F32)
    for p in range(DZ):
        part = r_ref[p * 32 : (p + 1) * 32, :]
        lo += jnp.where(p < e, part, 0.0)
        hi += jnp.where(p > e, part, 0.0)
    top = (e // 4) == 1
    at = lax.rem(e, 4)
    power = lambda k: jnp.where(k == 0, 1.0, jnp.where(k == 1, STEP_Z, jnp.where(k == 2, STEP_Z**2, STEP_Z**3)))
    up = jnp.where(top, power(at), 0.0)
    down = jnp.where(top, 0.0, power(3 - at))
    for load in loads:
        load.wait()
    tg, tm = tg_ref[...], tm_ref[...]
    ga = jnp.broadcast_to(tg[:, 0:1], (16, 128))
    gb = jnp.broadcast_to(tg[:, 1:2], (16, 128))
    for t in range(NX // 128):
        cols = slice(t * 128, (t + 1) * 128)
        cl[:, cols] = (pre_ref[0, :, cols] + up * x_ref[:, cols]) + (ga * lo[t : t + 1] + gb * lo[16 + t : 17 + t])
        ch[:, cols] = (pre_ref[1, :, cols] + down * x_ref[:, cols]) + (ga * hi[t : t + 1] + gb * hi[16 + t : 17 + t])
    hl = jnp.broadcast_to(tm[:8, 8:9], (8, NX))
    hh = jnp.broadcast_to(tm[:8, 9:10], (8, NX))
    stores = []
    for l in range(LY):
        o_ref[l] = (loc_ref[l] + scal_ref[d, l] * dz_ref[0] + scal_ref[d, 16 + l] * dz_ref[1]
                    + (hl * cl[l : l + 1, :] + hh * ch[l : l + 1, :]))
        if l % 4 == 3:
            i = l // 4
            stores += start((o_ref.at[pl.ds(l - 3, 4)], o_hbm.at[pl.ds(l - 3, 4)], sems.at[2 + i]))
    for store in stores:
        store.wait()


VMEM = pl.BlockSpec(memory_space=pltpu.VMEM)
SMEM = pl.BlockSpec(memory_space=pltpu.SMEM)
HBM = pl.BlockSpec(memory_space=pltpu.HBM)


def call(kernel, outs, ins, out_specs, scratch, mib, name):
    return pl.pallas_call(
        kernel,
        out_shape=tuple(jax.ShapeDtypeStruct(shape, F32) for shape in outs),
        in_specs=ins,
        out_specs=tuple(out_specs),
        scratch_shapes=scratch,
        compiler_params=pltpu.CompilerParams(vmem_limit_bytes=mib * 2**20),
        name=name,
    )


def pairs(count, odd):
    out = []
    for i in range(count):
        j = i + 1 if (i % 2 == 1) == odd else i - 1
        if 0 <= j < count:
            out.append((i, j))
    return out


def across(value, bit):
    return lax.ppermute(value, "gz", [(i, i ^ bit) for i in range(DZ)])


def on_device(temp, vel):
    rows = LY * LZ
    dma = pltpu.SemaphoreType.DMA
    temp, y1, y2, z1, z2 = call(
        faces_kernel, [(LY, LZ, NX), (LZ, NX), (LZ, NX), (LY, NX), (LY, NX)], [HBM], [VMEM] * 5, [dma], 8, "faces"
    )(temp)
    y1 = lax.ppermute(y1, "gy", pairs(DY, False))
    y2 = lax.ppermute(y2, "gy", pairs(DY, True))
    z1 = lax.ppermute(z1, "gz", pairs(DZ, False))
    z2 = lax.ppermute(z2, "gz", pairs(DZ, True))
    loc, a, c = call(
        local_kernel,
        [(LY, LZ, NX), (256, 128), (2, LY, NX)],
        [VMEM, HBM] + [VMEM] * 4 + [HBM] * 2,
        [VMEM] * 3,
        [
            pltpu.VMEM((NB, rows, XB), BF16),
            pltpu.VMEM((NB, rows, XB), BF16),
            pltpu.VMEM((NB, rows, XB), F32),
            pltpu.VMEM((2 * rows, NX), BF16),
            pltpu.VMEM((3, LY, LZ, NX), BF16),
            pltpu.VMEM((24, 128), F32),
            pltpu.VMEM((24, 128), F32),
            pltpu.VMEM((2, XB, XB), BF16),
            dma((4,)),
        ],
        16,
        "local",
    )(temp, vel, y1, y2, z1, z2, LINES, WX)
    x1 = across(c, 1)
    r1 = lax.all_to_all(a.reshape(DY, 8, 128), "gy", 0, 0)
    scanned, tot, pre = call(
        scan_kernel, [(DY, 8, 128), (2, LY, NX), (2, LY, NX)], [VMEM] * 3, [VMEM] * 3, [], 8, "scan"
    )(r1, c, x1)
    x2 = across(tot, 2)
    r2 = lax.all_to_all(scanned, "gy", 0, 0)
    dz, s, send, pre = call(
        mixed_kernel,
        [(2, LZ, NX), (256, 128), (LY, NX), (2, LY, NX)],
        [VMEM] * 4 + [HBM],
        [VMEM] * 4,
        [pltpu.VMEM((16, 128), F32), dma],
        8,
        "mixed",
    )(r2.reshape(256, 128), tot, x2, pre, SUMS)
    x3 = across(send, 4)
    r3 = lax.all_to_all(s.reshape(DZ, 32, 128), "gz", 0, 0)
    return call(
        final_kernel,
        [(LY, LZ, NX)],
        [VMEM] * 5 + [HBM, SMEM],
        [HBM],
        [
            pltpu.VMEM((LY, NX), F32),
            pltpu.VMEM((LY, NX), F32),
            pltpu.VMEM((LY, LZ, NX), F32),
            pltpu.VMEM((16, 128), F32),
            pltpu.VMEM((16, 128), F32),
            dma((6,)),
        ],
        16,
        "final",
    )(loc, dz, pre, x3, r3.reshape(256, 128), SUMS, SCAL)[0]


def solution(mesh):
    return jax.shard_map(
        on_device,
        mesh=mesh,
        in_specs=(P("gy", "gz", None), P(None, "gy", "gz", None)),
        out_specs=P("gy", "gz", None),
        check_vma=False,
    )
```

```python
import jax
import jax.numpy as jnp
import numpy as np
from jax import lax
from jax.experimental import pallas as pl
from jax.experimental.pallas import tpu as pltpu
from jax.sharding import PartitionSpec as P

NX, NY, NZ = 2048, 512, 64
RX, RY, RZ = 1, 768, 192
DY, DZ = 32, 8
GX, GZ = 4, 8
Q = NX // GX
LY, LZ = NY // DY, NZ // DZ
XB = 256
NB = NX // XB
KAPPA = 0.15
F32, BF16 = jnp.float32, jnp.bfloat16


def decay(ratio):
    half = 0.5 / ratio
    return 1.0 + half - np.sqrt(half * (2.0 + half))


def line_factors(count, ratio):
    q = decay(ratio)
    i = np.arange(count)
    low = 1.0 - q ** (2.0 * (i + 1))
    high = 1.0 - q ** (2.0 * (count - i))
    denom = ratio * (1.0 - q * q) * (1.0 - q ** (2.0 * count + 2))
    return q, low, high, denom


def split_line(count, ratio, parts):
    q, low, high, denom = line_factors(count, ratio)
    size = count // parts
    low, high = low.reshape(parts, size), high.reshape(parts, size)
    m = np.arange(size)
    small = np.minimum(m[:, None], m[None])
    large = np.maximum(m[:, None], m[None])
    block = q ** (large - small + 1.0) * low[:, small] * high[:, large] / denom
    up = q ** (size - 1.0 - m) * low
    down = q ** (1.0 * m) * high
    from_low = q ** (m + 2.0) * high / denom
    from_high = q ** (size + 1.0 - m) * low / denom
    return block, up, down, from_low, from_high, q**size


QX, QY, QZ = decay(RX), decay(RY), decay(RZ)


def tables():
    block_y, up_y, down_y, gl_y, gh_y, step_y = split_line(NY, RY, DY)
    block_z, up_z, down_z, gl_z, gh_z, step_z = split_line(NZ, RZ, DZ)
    sums = np.zeros((DY + DZ, 16, 128))
    tm = sums[DY:]
    tm[:, :8, :8] = block_z
    for e in range(DZ):
        for p in range(DZ):
            if p > e:
                tm[e, 8 + p, :8] = up_z[e] * step_z ** (p - e - 1)
            if p < e:
                tm[e, 8 + p, :8] = down_z[e] * step_z ** (e - p - 1)
    tm[:, :8, 8] = gl_z
    tm[:, :8, 9] = gh_z
    sums[:DY, :, 0] = gl_y
    sums[:DY, :, 1] = gh_y
    scal = np.zeros((DY, 128))
    scal[:, :16] = gl_y
    scal[:, 16:32] = gh_y
    scal[:, 32:48] = up_y
    scal[:, 48:64] = down_y
    group = step_y**GX
    for d in range(DY):
        z, x = d // GX, d % GX
        for i in range(GX):
            xi = x ^ i
            scal[d, 64 + i] = step_y ** (GX - 1 - xi)
            scal[d, 68 + i] = step_y**xi
            for j in range(GX):
                xj = x ^ j
                if xj < xi:
                    scal[d, 80 + 4 * i + j] = step_y ** (xi - xj - 1)
                if xj > xi:
                    scal[d, 96 + 4 * i + j] = step_y ** (xj - xi - 1)
        for p in range(GZ):
            if p != z:
                scal[d, 72 + p] = group ** (abs(p - z) - 1)
    f32 = lambda a: a.astype(np.float32)
    return f32(sums), f32(scal), float(step_z)


SUMS, SCAL, STEP_Z = tables()
ROWS = LY * LZ


def halves(value):
    high = value.astype(BF16)
    return high, (value - high.astype(F32)).astype(BF16)


def mm(a, b):
    return jnp.dot(a, b, preferred_element_type=F32)


def start(*pairs_and_sem):
    copies = [pltpu.make_async_copy(*p) for p in pairs_and_sem]
    for c in copies:
        c.start()
    return copies


def power(q, k):
    return jnp.exp2(k * float(np.log2(q)))


def solve_x(high, low, wx_ref, g, put):
    lines = high.shape[1]
    wh, wl = wx_ref[0], wx_ref[1]
    xh = high[...].reshape(NB * lines, XB)
    xl = low[...].reshape(NB * lines, XB)
    g[...] = (mm(xh, wh) + (mm(xh, wl) + mm(xl, wh))).reshape(NB, lines, XB)
    lane = lax.broadcasted_iota(jnp.int32, (8, 128), 1).astype(F32)
    left, right = power(QX, lane + 1.0)[0:1], power(QX, 128.0 - lane)[0:1]
    for b in range(NB):
        before = g[b - 1, :, XB - 1 :] if b > 0 else g[0, :, :1] * (-QX)
        after = g[b + 1, :, :1] if b < NB - 1 else g[NB - 1, :, XB - 1 :] * (-QX)
        put(2 * b, g[b, :, :128] + before * left)
        put(2 * b + 1, g[b, :, 128:] + after * right)


def faces_kernel(t_ref, y1_ref, y2_ref, z1_ref, z2_ref):
    d, e = lax.axis_index("gy"), lax.axis_index("gz")
    odd_y, odd_z = (d % 2) == 1, (e % 2) == 1
    first, last = t_ref[0], t_ref[LY - 1]
    y1_ref[...] = jnp.where(odd_y, first, last)
    y2_ref[...] = jnp.where(odd_y, last, first)
    for y in range(LY):
        bottom, top = t_ref[y, 0:1, :], t_ref[y, LZ - 1 : LZ, :]
        z1_ref[y : y + 1, :] = jnp.where(odd_z, bottom, top)
        z2_ref[y : y + 1, :] = jnp.where(odd_z, top, bottom)


def inner_kernel(t_ref, v_ref, scal_ref, f_ref, mf_ref, ml_ref, wx_ref, tv_ref):
    d, e = lax.axis_index("gy"), lax.axis_index("gz")
    zi = lax.broadcasted_iota(jnp.int32, (LZ, NX), 0)
    xi = lax.broadcasted_iota(jnp.int32, (LZ, NX), 1)
    nothing = jnp.zeros((LZ, NX), F32)
    for y in range(LY):
        t = t_ref[y]
        north = t_ref[y + 1] if y < LY - 1 else nothing
        south = t_ref[y - 1] if y > 0 else nothing
        ceil = jnp.where(zi == LZ - 1, 0.0, pltpu.roll(t, LZ - 1, 0))
        floor = jnp.where(zi == 0, 0.0, pltpu.roll(t, 1, 0))
        east = jnp.where(xi == NX - 1, 0.0, pltpu.roll(t, NX - 1, 1))
        west = jnp.where(xi == 0, 0.0, pltpu.roll(t, 1, 1))
        lap = ((east + west) + (north + south)) + (ceil + floor) - 6.0 * t
        adv = (v_ref[0, y].astype(F32) * (east - west) + v_ref[1, y].astype(F32) * (north - south)
               + v_ref[2, y].astype(F32) * (ceil - floor))
        f_ref[y] = t + KAPPA * lap - 0.5 * adv
    i = lax.broadcasted_iota(jnp.int32, (XB, XB), 0)
    j = lax.broadcasted_iota(jnp.int32, (XB, XB), 1)
    w = power(QX, (jnp.abs(i - j) + 1).astype(F32)) * (1.0 / (RX * (1 - QX * QX)))
    wx_ref[0], wx_ref[1] = halves(w)
    row = scal_ref[pl.ds(d, 1), :]
    r = lax.broadcasted_iota(jnp.int32, (128, 128), 0)
    c = lax.broadcasted_iota(jnp.int32, (128, 128), 1)
    tv_ref[...] = jnp.broadcast_to(jnp.sum(jnp.where(r == c, row, 0.0), axis=1, keepdims=True), (128, 128))
    lane = lax.broadcasted_iota(jnp.int32, (16, 128), 1)
    sub = lax.broadcasted_iota(jnp.int32, (16, 128), 0)

    def block(q, ratio, count, first, own, other):
        small = (jnp.minimum(own, other) + first + 1).astype(F32)
        large = (count - first - jnp.maximum(own, other)).astype(F32)
        gap = (jnp.abs(own - other) + 1).astype(F32)
        return (power(q, gap) * (1.0 - power(q, 2.0 * small)) * (1.0 - power(q, 2.0 * large))
                * (1.0 / (ratio * (1 - q * q) * (1 - q ** (2.0 * count + 2)))))

    my = block(QY, RY, NY, d * LY, sub, lane // LZ)
    w8 = (lane % LZ)[:8]
    mz = block(QZ, RZ, NZ, e * LZ, sub[:8], w8)
    up = power(QZ, (LZ - 1 - w8).astype(F32)) * (1.0 - power(QZ, 2.0 * (w8 + e * LZ + 1).astype(F32)))
    down = power(QZ, w8.astype(F32)) * (1.0 - power(QZ, 2.0 * (NZ - e * LZ - w8).astype(F32)))
    for l in range(LY // 2):
        pair = jnp.concatenate([my[2 * l : 2 * l + 1] * mz, my[2 * l + 1 : 2 * l + 2] * mz], axis=0)
        high, low = halves(pair)
        mf_ref[16 * l : 16 * l + 16, :128] = high
        mf_ref[16 * l : 16 * l + 16, 128:] = high
        ml_ref[16 * l : 16 * l + 16] = low
    for k, part in ((0, up), (1, down)):
        high, low = halves(my * part[0:1])
        at = ROWS + 16 * k
        mf_ref[at : at + 16, :128] = high
        mf_ref[at : at + 16, 128:] = high
        ml_ref[at : at + 16] = low


def source_kernel(f0_ref, v_ref, y1_ref, y2_ref, z1_ref, z2_ref, wx_ref, tv_ref,
                  f_ref, own_ref, s1_ref, s2_ref, s3_ref, ah, al, g, a4):
    d, e = lax.axis_index("gy"), lax.axis_index("gz")
    odd_y, odd_z = (d % 2) == 1, (e % 2) == 1
    zi = lax.broadcasted_iota(jnp.int32, (LZ, XB), 0)
    for b in range(NB):
        cols = slice(b * XB, (b + 1) * XB)
        sums = [jnp.zeros((LZ, XB), F32), jnp.zeros((LZ, XB), F32)]
        for y in range(LY):
            f = f0_ref[y, :, cols]
            w = 0.5 * v_ref[2, y, :, cols].astype(F32)
            h1, h2 = z1_ref[y : y + 1, cols], z2_ref[y : y + 1, cols]
            above, below = jnp.where(odd_z, h2, h1), jnp.where(odd_z, h1, h2)
            f += jnp.where(zi == 0, (KAPPA + w) * below, jnp.where(zi == LZ - 1, (KAPPA - w) * above, 0.0))
            if y == 0:
                south = jnp.where(odd_y, y1_ref[:, cols], y2_ref[:, cols])
                f += (KAPPA + 0.5 * v_ref[1, y, :, cols].astype(F32)) * south
            if y == LY - 1:
                north = jnp.where(odd_y, y2_ref[:, cols], y1_ref[:, cols])
                f += (KAPPA - 0.5 * v_ref[1, y, :, cols].astype(F32)) * north
            f_ref[y, :, cols] = f
            for k in range(2):
                c = tv_ref[32 + 16 * k + y : 33 + 16 * k + y, :]
                sums[k] += f * jnp.concatenate([c, c], axis=1)
        high, low = halves(jnp.concatenate(sums, axis=0))
        ah[b] = high
        al[b] = low

    def put(t, part):
        for k in range(2):
            a4[t // 4, k, :, (t % 4) * 128 : (t % 4 + 1) * 128] = part[8 * k : 8 * k + 8]

    solve_x(ah, al, wx_ref, g, put)
    x = lax.rem(d, GX)
    for i, ref in enumerate((own_ref, s1_ref, s2_ref, s3_ref)):
        ref[...] = a4[lax.bitwise_xor(x, i)]


def local_kernel(f_ref, wx_ref, mf_ref, ml_ref, loc_ref, c_ref, fh, fl, g, ghl):
    for b in range(NB):
        high, low = halves(f_ref[:, :, b * XB : (b + 1) * XB].reshape(ROWS, XB))
        fh[b] = high
        fl[b] = low

    def put(t, part):
        high, low = halves(part)
        ghl[:ROWS, t * 128 : (t + 1) * 128] = high
        ghl[ROWS:, t * 128 : (t + 1) * 128] = low

    solve_x(fh, fl, wx_ref, g, put)
    for b in range(NB):
        cols = slice(b * XB, (b + 1) * XB)
        out = mm(mf_ref[...], ghl[:, cols]) + mm(ml_ref[...], ghl[:ROWS, cols])
        loc_ref[:, :, cols] = out[:ROWS].reshape(LY, LZ, XB)
        c_ref[0, :, cols] = out[ROWS : ROWS + 16]
        c_ref[1, :, cols] = out[ROWS + 16 :]


def group_kernel(a_ref, b_ref, c_ref, d_ref, tv_ref, o_ref):
    z = lax.axis_index("gy") // GX
    parts = (a_ref, b_ref, c_ref, d_ref)
    for t in range(Q // 128):
        cols = slice(t * 128, (t + 1) * 128)
        tot = []
        for k in range(2):
            base = 64 + 4 * k
            tot.append(sum(tv_ref[base + i : base + i + 1, :] * parts[i][k, :, cols] for i in range(4)))
        for p in range(GZ):
            o_ref[p, :, cols] = tv_ref[72 + p : 73 + p, :] * jnp.where(p > z, tot[0], tot[1])


def spread_kernel(a_ref, b_ref, c_ref, d_ref, r_ref, tv_ref, cs_ref, x_ref,
                  own_ref, s1_ref, s2_ref, s3_ref, tot_ref, pre_ref):
    d, e = lax.axis_index("gy"), lax.axis_index("gz")
    z = d // GX
    parts = (a_ref, b_ref, c_ref, d_ref)
    outs = (own_ref, s1_ref, s2_ref, s3_ref)
    for t in range(Q // 128):
        cols = slice(t * 128, (t + 1) * 128)
        low = jnp.zeros((8, 128), F32)
        high = jnp.zeros((8, 128), F32)
        for p in range(GZ):
            part = r_ref[p, :, cols]
            low += jnp.where(p < z, part, 0.0)
            high += jnp.where(p > z, part, 0.0)
        for k, group in ((0, low), (1, high)):
            vals = [ref[k, :, cols] for ref in parts]
            for i in range(4):
                at = 68 + i if k == 0 else 64 + i
                total = tv_ref[at : at + 1, :] * group
                for j in range(4):
                    if j != i:
                        row = 80 + 16 * k + 4 * i + j
                        total += tv_ref[row : row + 1, :] * vals[j]
                outs[i][k, :, cols] = total
    upper = (e % 2) == 1
    near, far = jnp.where(upper, 1.0, STEP_Z), jnp.where(upper, STEP_Z, 1.0)
    tot_ref[0] = near * cs_ref[0] + far * x_ref[0]
    tot_ref[1] = far * cs_ref[1] + near * x_ref[1]
    pre_ref[0] = jnp.where(upper, x_ref[0], 0.0)
    pre_ref[1] = jnp.where(upper, 0.0, x_ref[1])


def mixed_kernel(p0_ref, p1_ref, p2_ref, p3_ref, tot_ref, x_ref, pre_ref, sums_hbm,
                 dz_ref, s_ref, send_ref, pre2_ref, p4, tm_ref, sem):
    e = lax.axis_index("gz")
    load = pltpu.make_async_copy(sums_hbm.at[DY + e], tm_ref, sem)
    load.start()
    x = lax.rem(lax.axis_index("gy"), GX)
    for i, ref in enumerate((p0_ref, p1_ref, p2_ref, p3_ref)):
        p4[lax.bitwise_xor(x, i)] = ref[...]
    upper = ((e // 2) % 2) == 1
    odd = (e % 2) == 1
    two = STEP_Z * STEP_Z
    near, far = jnp.where(upper, 1.0, two), jnp.where(upper, two, 1.0)
    top = (e // 4) == 1
    send_ref[...] = jnp.where(top, far * tot_ref[1] + near * x_ref[1], near * tot_ref[0] + far * x_ref[0])
    low = jnp.where(odd, STEP_Z, 1.0)
    high = jnp.where(odd, 1.0, STEP_Z)
    pre2_ref[0] = pre_ref[0] + jnp.where(upper, low * x_ref[0], 0.0)
    pre2_ref[1] = pre_ref[1] + jnp.where(upper, 0.0, high * x_ref[1])
    load.wait()
    tm = tm_ref[...]
    own = [jnp.broadcast_to(tm[:8, w : w + 1], (8, 128)) for w in range(8)]
    out = [jnp.broadcast_to(tm[8:, w : w + 1], (8, 128)) for w in range(8)]
    for k in range(2):
        for t in range(16):
            p = p4[t // 4, k, :, (t % 4) * 128 : (t % 4 + 1) * 128]
            one = own[0] * p[0:1]
            two = out[0] * p[0:1]
            for w in range(1, 8):
                one += own[w] * p[w : w + 1]
                two += out[w] * p[w : w + 1]
            dz_ref[k, :, t * 128 : (t + 1) * 128] = one
            s_ref[pl.ds(k * 16 + t, 8, stride=32), :] = two


def final_kernel(loc_ref, dz_ref, pre_ref, x_ref, r_ref, sums_hbm, tv_ref, o_hbm,
                 cl, ch, o_ref, tg_ref, tm_ref, sems):
    d, e = lax.axis_index("gy"), lax.axis_index("gz")
    loads = start((sums_hbm.at[d], tg_ref, sems.at[0]), (sums_hbm.at[DY + e], tm_ref, sems.at[1]))
    lo = jnp.zeros((32, 128), F32)
    hi = jnp.zeros((32, 128), F32)
    for p in range(DZ):
        part = r_ref[p * 32 : (p + 1) * 32, :]
        lo += jnp.where(p < e, part, 0.0)
        hi += jnp.where(p > e, part, 0.0)
    top = (e // 4) == 1
    at = lax.rem(e, 4)
    power = lambda k: jnp.where(k == 0, 1.0, jnp.where(k == 1, STEP_Z, jnp.where(k == 2, STEP_Z**2, STEP_Z**3)))
    up = jnp.where(top, power(at), 0.0)
    down = jnp.where(top, 0.0, power(3 - at))
    for load in loads:
        load.wait()
    tg, tm = tg_ref[...], tm_ref[...]
    ga = jnp.broadcast_to(tg[:, 0:1], (16, 128))
    gb = jnp.broadcast_to(tg[:, 1:2], (16, 128))
    for t in range(NX // 128):
        cols = slice(t * 128, (t + 1) * 128)
        cl[:, cols] = (pre_ref[0, :, cols] + up * x_ref[:, cols]) + (ga * lo[t : t + 1] + gb * lo[16 + t : 17 + t])
        ch[:, cols] = (pre_ref[1, :, cols] + down * x_ref[:, cols]) + (ga * hi[t : t + 1] + gb * hi[16 + t : 17 + t])
    hl = jnp.broadcast_to(tm[:8, 8:9], (8, 128))
    hh = jnp.broadcast_to(tm[:8, 9:10], (8, 128))
    stores = []
    for l in range(LY):
        for t in range(NX // 128):
            cols = slice(t * 128, (t + 1) * 128)
            o_ref[l, :, cols] = (
                loc_ref[l, :, cols] + tv_ref[l : l + 1, :] * dz_ref[0, :, cols]
                + tv_ref[16 + l : 17 + l, :] * dz_ref[1, :, cols]
                + (hl * cl[l : l + 1, cols] + hh * ch[l : l + 1, cols]))
        if l % 4 == 3:
            i = l // 4
            stores += start((o_ref.at[pl.ds(l - 3, 4)], o_hbm.at[pl.ds(l - 3, 4)], sems.at[2 + i]))
    for store in stores:
        store.wait()


VMEM = pl.BlockSpec(memory_space=pltpu.VMEM)
HBM = pl.BlockSpec(memory_space=pltpu.HBM)
FULL, QUARTER, SUMS_Z = (LY, LZ, NX), (2, LZ, Q), (2, LY, NX)


def call(kernel, outs, ins, out_specs, scratch, mib, name, cost=None):
    if cost is not None:
        cost = pl.CostEstimate(flops=cost[0], bytes_accessed=cost[1], transcendentals=0)
    return pl.pallas_call(
        kernel,
        out_shape=tuple(o if isinstance(o, jax.ShapeDtypeStruct) else jax.ShapeDtypeStruct(o, F32) for o in outs),
        in_specs=ins,
        out_specs=tuple(out_specs),
        scratch_shapes=scratch,
        compiler_params=pltpu.CompilerParams(vmem_limit_bytes=mib * 2**20),
        cost_estimate=cost,
        name=name,
    )


def pairs(count, odd):
    out = []
    for i in range(count):
        j = i + 1 if (i % 2 == 1) == odd else i - 1
        if 0 <= j < count:
            out.append((i, j))
    return out


def across(value, axis, count, bit):
    return lax.ppermute(value, axis, [(i, i ^ bit) for i in range(count)])


COLUMN = [[z * GX + x for z in range(GZ)] for x in range(GX)]


def on_device(temp, vel):
    dma = pltpu.SemaphoreType.DMA
    bf = lambda *shape: jax.ShapeDtypeStruct(shape, BF16)
    y1, y2, z1, z2 = call(
        faces_kernel, [(LZ, NX), (LZ, NX), (LY, NX), (LY, NX)], [VMEM], [VMEM] * 4, [], 4, "faces"
    )(temp)
    y1 = lax.ppermute(y1, "gy", pairs(DY, False))
    y2 = lax.ppermute(y2, "gy", pairs(DY, True))
    z1 = lax.ppermute(z1, "gz", pairs(DZ, False))
    z2 = lax.ppermute(z2, "gz", pairs(DZ, True))
    f, mf, ml, wx, tv = call(
        inner_kernel,
        [FULL, bf(ROWS + 32, 256), bf(ROWS + 32, 128), bf(2, XB, XB), (128, 128)],
        [VMEM] * 3,
        [VMEM] * 5,
        [],
        16,
        "inner",
        (10**7, 8 * 10**6),
    )(temp, vel, SCAL)
    f, *mine = call(
        source_kernel,
        [FULL] + [QUARTER] * 4,
        [VMEM] * 8,
        [VMEM] * 5,
        [
            pltpu.VMEM((NB, 16, XB), BF16),
            pltpu.VMEM((NB, 16, XB), BF16),
            pltpu.VMEM((NB, 16, XB), F32),
            pltpu.VMEM((GX, 2, LZ, Q), F32),
        ],
        16,
        "source",
    )(f, vel, y1, y2, z1, z2, wx, tv)
    sets = [mine[0]] + [across(mine[i], "gy", DY, i) for i in (1, 2, 3)]
    loc, c = call(
        local_kernel,
        [FULL, SUMS_Z],
        [VMEM] * 4,
        [VMEM] * 2,
        [
            pltpu.VMEM((NB, ROWS, XB), BF16),
            pltpu.VMEM((NB, ROWS, XB), BF16),
            pltpu.VMEM((NB, ROWS, XB), F32),
            pltpu.VMEM((2 * ROWS, NX), BF16),
        ],
        16,
        "local",
        (2 * 10**9, 8 * 10**6),
    )(f, wx, mf, ml)
    x1 = across(c, "gz", DZ, 1)
    tots = call(group_kernel, [(GZ, LZ, Q)], [VMEM] * 5, [VMEM], [], 4, "group")(*sets, tv)[0]
    r1 = lax.all_to_all(tots, "gy", 0, 0, axis_index_groups=COLUMN)
    *mine, tot, pre = call(
        spread_kernel, [QUARTER] * 4 + [SUMS_Z] * 2, [VMEM] * 8, [VMEM] * 6, [], 8, "spread"
    )(*sets, r1, tv, c, x1)
    sets = [mine[0]] + [across(mine[i], "gy", DY, i) for i in (1, 2, 3)]
    x2 = across(tot, "gz", DZ, 2)
    dz, s, send, pre = call(
        mixed_kernel,
        [(2, LZ, NX), (256, 128), (LY, NX), SUMS_Z],
        [VMEM] * 7 + [HBM],
        [VMEM] * 4,
        [pltpu.VMEM((GX, 2, LZ, Q), F32), pltpu.VMEM((16, 128), F32), dma],
        8,
        "mixed",
    )(*sets, tot, x2, pre, SUMS)
    x3 = across(send, "gz", DZ, 4)
    r3 = lax.all_to_all(s.reshape(DZ, 32, 128), "gz", 0, 0)
    return call(
        final_kernel,
        [FULL],
        [VMEM] * 5 + [HBM, VMEM],
        [HBM],
        [
            pltpu.VMEM((LY, NX), F32),
            pltpu.VMEM((LY, NX), F32),
            pltpu.VMEM(FULL, F32),
            pltpu.VMEM((16, 128), F32),
            pltpu.VMEM((16, 128), F32),
            dma((6,)),
        ],
        16,
        "final",
    )(loc, dz, pre, x3, r3.reshape(256, 128), SUMS, tv)[0]


def solution(mesh):
    return jax.shard_map(
        on_device,
        mesh=mesh,
        in_specs=(P("gy", "gz", None), P(None, "gy", "gz", None)),
        out_specs=P("gy", "gz", None),
        check_vma=False,
    )
```

```python
import jax
import jax.numpy as jnp
import numpy as np
from jax import lax
from jax.experimental import pallas as pl
from jax.experimental.pallas import tpu as pltpu
from jax.sharding import PartitionSpec as P

NX, NY, NZ = 2048, 512, 64
RX, RY, RZ = 1, 768, 192
DY, DZ = 32, 8
GX, GZ = 4, 8
Q = NX // GX
LY, LZ = NY // DY, NZ // DZ
XB = 256
NB = NX // XB
KAPPA = 0.15
F32, BF16 = jnp.float32, jnp.bfloat16


def decay(ratio):
    half = 0.5 / ratio
    return 1.0 + half - np.sqrt(half * (2.0 + half))


def line_factors(count, ratio):
    q = decay(ratio)
    i = np.arange(count)
    low = 1.0 - q ** (2.0 * (i + 1))
    high = 1.0 - q ** (2.0 * (count - i))
    denom = ratio * (1.0 - q * q) * (1.0 - q ** (2.0 * count + 2))
    return q, low, high, denom


def split_line(count, ratio, parts):
    q, low, high, denom = line_factors(count, ratio)
    size = count // parts
    low, high = low.reshape(parts, size), high.reshape(parts, size)
    m = np.arange(size)
    small = np.minimum(m[:, None], m[None])
    large = np.maximum(m[:, None], m[None])
    block = q ** (large - small + 1.0) * low[:, small] * high[:, large] / denom
    up = q ** (size - 1.0 - m) * low
    down = q ** (1.0 * m) * high
    from_low = q ** (m + 2.0) * high / denom
    from_high = q ** (size + 1.0 - m) * low / denom
    return block, up, down, from_low, from_high, q**size


QX, QY, QZ = decay(RX), decay(RY), decay(RZ)


def tables():
    block_y, up_y, down_y, gl_y, gh_y, step_y = split_line(NY, RY, DY)
    block_z, up_z, down_z, gl_z, gh_z, step_z = split_line(NZ, RZ, DZ)
    sums = np.zeros((DY + DZ, 16, 128))
    tm = sums[DY:]
    tm[:, :8, :8] = block_z
    for e in range(DZ):
        for p in range(DZ):
            if p > e:
                tm[e, 8 + p, :8] = up_z[e] * step_z ** (p - e - 1)
            if p < e:
                tm[e, 8 + p, :8] = down_z[e] * step_z ** (e - p - 1)
    tm[:, :8, 8] = gl_z
    tm[:, :8, 9] = gh_z
    sums[:DY, :, 0] = gl_y
    sums[:DY, :, 1] = gh_y
    scal = np.zeros((DY, 128))
    scal[:, :16] = gl_y
    scal[:, 16:32] = gh_y
    scal[:, 32:48] = up_y
    scal[:, 48:64] = down_y
    group = step_y**GX
    for d in range(DY):
        z, x = d // GX, d % GX
        for i in range(GX):
            xi = x ^ i
            scal[d, 64 + i] = step_y ** (GX - 1 - xi)
            scal[d, 68 + i] = step_y**xi
            for j in range(GX):
                xj = x ^ j
                if xj < xi:
                    scal[d, 80 + 4 * i + j] = step_y ** (xi - xj - 1)
                if xj > xi:
                    scal[d, 96 + 4 * i + j] = step_y ** (xj - xi - 1)
        for p in range(GZ):
            if p != z:
                scal[d, 72 + p] = group ** (abs(p - z) - 1)
    f32 = lambda a: a.astype(np.float32)
    return f32(sums), f32(scal), float(step_z)


SUMS, SCAL, STEP_Z = tables()
ROWS = LY * LZ


def halves(value):
    high = value.astype(BF16)
    return high, (value - high.astype(F32)).astype(BF16)


def mm(a, b):
    return jnp.dot(a, b, preferred_element_type=F32)


def start(*pairs_and_sem):
    copies = [pltpu.make_async_copy(*p) for p in pairs_and_sem]
    for c in copies:
        c.start()
    return copies


def power(q, k):
    return jnp.exp2(k * float(np.log2(q)))


def solve_x(high, low, wx_ref, g, put):
    lines = high.shape[1]
    wh, wl = wx_ref[0], wx_ref[1]
    xh = high[...].reshape(NB * lines, XB)
    xl = low[...].reshape(NB * lines, XB)
    g[...] = (mm(xh, wh) + (mm(xh, wl) + mm(xl, wh))).reshape(NB, lines, XB)
    lane = lax.broadcasted_iota(jnp.int32, (8, 128), 1).astype(F32)
    left, right = power(QX, lane + 1.0)[0:1], power(QX, 128.0 - lane)[0:1]
    for b in range(NB):
        before = g[b - 1, :, XB - 1 :] if b > 0 else g[0, :, :1] * (-QX)
        after = g[b + 1, :, :1] if b < NB - 1 else g[NB - 1, :, XB - 1 :] * (-QX)
        put(2 * b, g[b, :, :128] + before * left)
        put(2 * b + 1, g[b, :, 128:] + after * right)


def faces_kernel(t_ref, y1_ref, y2_ref, z1_ref, z2_ref):
    d, e = lax.axis_index("gy"), lax.axis_index("gz")
    odd_y, odd_z = (d % 2) == 1, (e % 2) == 1
    first, last = t_ref[0], t_ref[LY - 1]
    y1_ref[...] = jnp.where(odd_y, first, last)
    y2_ref[...] = jnp.where(odd_y, last, first)
    for y in range(LY):
        bottom, top = t_ref[y, 0:1, :], t_ref[y, LZ - 1 : LZ, :]
        z1_ref[y : y + 1, :] = jnp.where(odd_z, bottom, top)
        z2_ref[y : y + 1, :] = jnp.where(odd_z, top, bottom)


def inner_kernel(t_ref, v_ref, scal_ref, f_ref, mf_ref, ml_ref, wx_ref, tv_ref):
    d, e = lax.axis_index("gy"), lax.axis_index("gz")
    zi = lax.broadcasted_iota(jnp.int32, (LZ, NX), 0)
    xi = lax.broadcasted_iota(jnp.int32, (LZ, NX), 1)
    nothing = jnp.zeros((LZ, NX), F32)
    for y in range(LY):
        t = t_ref[y]
        north = t_ref[y + 1] if y < LY - 1 else nothing
        south = t_ref[y - 1] if y > 0 else nothing
        ceil = jnp.where(zi == LZ - 1, 0.0, pltpu.roll(t, LZ - 1, 0))
        floor = jnp.where(zi == 0, 0.0, pltpu.roll(t, 1, 0))
        east = jnp.where(xi == NX - 1, 0.0, pltpu.roll(t, NX - 1, 1))
        west = jnp.where(xi == 0, 0.0, pltpu.roll(t, 1, 1))
        lap = ((east + west) + (north + south)) + (ceil + floor) - 6.0 * t
        adv = (v_ref[0, y].astype(F32) * (east - west) + v_ref[1, y].astype(F32) * (north - south)
               + v_ref[2, y].astype(F32) * (ceil - floor))
        f_ref[y] = t + KAPPA * lap - 0.5 * adv
    i = lax.broadcasted_iota(jnp.int32, (XB, XB), 0)
    j = lax.broadcasted_iota(jnp.int32, (XB, XB), 1)
    w = power(QX, (jnp.abs(i - j) + 1).astype(F32)) * (1.0 / (RX * (1 - QX * QX)))
    wx_ref[0], wx_ref[1] = halves(w)
    row = scal_ref[pl.ds(d, 1), :]
    r = lax.broadcasted_iota(jnp.int32, (128, 128), 0)
    c = lax.broadcasted_iota(jnp.int32, (128, 128), 1)
    tv_ref[...] = jnp.broadcast_to(jnp.sum(jnp.where(r == c, row, 0.0), axis=1, keepdims=True), (128, 128))
    lane = lax.broadcasted_iota(jnp.int32, (16, 128), 1)
    sub = lax.broadcasted_iota(jnp.int32, (16, 128), 0)

    def block(q, ratio, count, first, own, other):
        small = (jnp.minimum(own, other) + first + 1).astype(F32)
        large = (count - first - jnp.maximum(own, other)).astype(F32)
        gap = (jnp.abs(own - other) + 1).astype(F32)
        return (power(q, gap) * (1.0 - power(q, 2.0 * small)) * (1.0 - power(q, 2.0 * large))
                * (1.0 / (ratio * (1 - q * q) * (1 - q ** (2.0 * count + 2)))))

    my = block(QY, RY, NY, d * LY, sub, lane // LZ)
    w8 = (lane % LZ)[:8]
    mz = block(QZ, RZ, NZ, e * LZ, sub[:8], w8)
    up = power(QZ, (LZ - 1 - w8).astype(F32)) * (1.0 - power(QZ, 2.0 * (w8 + e * LZ + 1).astype(F32)))
    down = power(QZ, w8.astype(F32)) * (1.0 - power(QZ, 2.0 * (NZ - e * LZ - w8).astype(F32)))
    for l in range(LY // 2):
        pair = jnp.concatenate([my[2 * l : 2 * l + 1] * mz, my[2 * l + 1 : 2 * l + 2] * mz], axis=0)
        high, low = halves(pair)
        mf_ref[16 * l : 16 * l + 16, :128] = high
        mf_ref[16 * l : 16 * l + 16, 128:] = high
        ml_ref[16 * l : 16 * l + 16] = low
    for k, part in ((0, up), (1, down)):
        high, low = halves(my * part[0:1])
        at = ROWS + 16 * k
        mf_ref[at : at + 16, :128] = high
        mf_ref[at : at + 16, 128:] = high
        ml_ref[at : at + 16] = low


def source_kernel(f0_ref, v_ref, y1_ref, y2_ref, z1_ref, z2_ref, wx_ref, tv_ref,
                  f_ref, own_ref, s1_ref, s2_ref, s3_ref, ah, al, g, a4):
    d, e = lax.axis_index("gy"), lax.axis_index("gz")
    odd_y, odd_z = (d % 2) == 1, (e % 2) == 1
    zi = lax.broadcasted_iota(jnp.int32, (LZ, XB), 0)
    for b in range(NB):
        cols = slice(b * XB, (b + 1) * XB)
        sums = [jnp.zeros((LZ, XB), F32), jnp.zeros((LZ, XB), F32)]
        for y in range(LY):
            f = f0_ref[y, :, cols]
            w = 0.5 * v_ref[2, y, :, cols].astype(F32)
            h1, h2 = z1_ref[y : y + 1, cols], z2_ref[y : y + 1, cols]
            above, below = jnp.where(odd_z, h2, h1), jnp.where(odd_z, h1, h2)
            f += jnp.where(zi == 0, (KAPPA + w) * below, jnp.where(zi == LZ - 1, (KAPPA - w) * above, 0.0))
            if y == 0:
                south = jnp.where(odd_y, y1_ref[:, cols], y2_ref[:, cols])
                f += (KAPPA + 0.5 * v_ref[1, y, :, cols].astype(F32)) * south
            if y == LY - 1:
                north = jnp.where(odd_y, y2_ref[:, cols], y1_ref[:, cols])
                f += (KAPPA - 0.5 * v_ref[1, y, :, cols].astype(F32)) * north
            f_ref[y, :, cols] = f
            for k in range(2):
                c = tv_ref[32 + 16 * k + y : 33 + 16 * k + y, :]
                sums[k] += f * jnp.concatenate([c, c], axis=1)
        high, low = halves(jnp.concatenate(sums, axis=0))
        ah[b] = high
        al[b] = low

    def put(t, part):
        for k in range(2):
            a4[t // 4, k, :, (t % 4) * 128 : (t % 4 + 1) * 128] = part[8 * k : 8 * k + 8]

    solve_x(ah, al, wx_ref, g, put)
    x = lax.rem(d, GX)
    for i, ref in enumerate((own_ref, s1_ref, s2_ref, s3_ref)):
        ref[...] = a4[lax.bitwise_xor(x, i)]


def local_kernel(f_ref, wx_ref, mf_ref, ml_ref, loc_ref, c_ref, fh, fl, g, ghl):
    for b in range(NB):
        high, low = halves(f_ref[:, :, b * XB : (b + 1) * XB].reshape(ROWS, XB))
        fh[b] = high
        fl[b] = low

    def put(t, part):
        high, low = halves(part)
        ghl[:ROWS, t * 128 : (t + 1) * 128] = high
        ghl[ROWS:, t * 128 : (t + 1) * 128] = low

    solve_x(fh, fl, wx_ref, g, put)
    for b in range(NB):
        cols = slice(b * XB, (b + 1) * XB)
        out = mm(mf_ref[...], ghl[:, cols]) + mm(ml_ref[...], ghl[:ROWS, cols])
        loc_ref[:, :, cols] = out[:ROWS].reshape(LY, LZ, XB)
        c_ref[0, :, cols] = out[ROWS : ROWS + 16]
        c_ref[1, :, cols] = out[ROWS + 16 :]


def group_kernel(a_ref, b_ref, c_ref, d_ref, tv_ref, o_ref):
    z = lax.axis_index("gy") // GX
    parts = (a_ref, b_ref, c_ref, d_ref)
    for t in range(Q // 128):
        cols = slice(t * 128, (t + 1) * 128)
        tot = []
        for k in range(2):
            base = 64 + 4 * k
            tot.append(sum(tv_ref[base + i : base + i + 1, :] * parts[i][k, :, cols] for i in range(4)))
        for p in range(GZ):
            o_ref[p, :, cols] = tv_ref[72 + p : 73 + p, :] * jnp.where(p > z, tot[0], tot[1])


def weights(sums_ref, first):
    tm = sums_ref[DY + lax.axis_index("gz")]
    return [jnp.broadcast_to(tm[first : first + 8, w : w + 1], (8, 128)) for w in range(8)]


def weighted(rows, p):
    total = rows[0] * p[0:1]
    for w in range(1, 8):
        total += rows[w] * p[w : w + 1]
    return total


def spread_kernel(a_ref, b_ref, c_ref, d_ref, r_ref, tv_ref, sums_ref, own_ref, s1_ref, s2_ref, s3_ref, o_ref):
    d = lax.axis_index("gy")
    z, x = d // GX, lax.rem(d, GX)
    out = weights(sums_ref, 8)
    parts = (a_ref, b_ref, c_ref, d_ref)
    outs = (own_ref, s1_ref, s2_ref, s3_ref)
    for t in range(Q // 128):
        cols = slice(t * 128, (t + 1) * 128)
        low = jnp.zeros((8, 128), F32)
        high = jnp.zeros((8, 128), F32)
        for p in range(GZ):
            part = r_ref[p, :, cols]
            low += jnp.where(p < z, part, 0.0)
            high += jnp.where(p > z, part, 0.0)
        for k, group in ((0, low), (1, high)):
            vals = [ref[k, :, cols] for ref in parts]
            for i in range(4):
                at = 68 + i if k == 0 else 64 + i
                total = tv_ref[at : at + 1, :] * group
                for j in range(4):
                    if j != i:
                        row = 80 + 16 * k + 4 * i + j
                        total += tv_ref[row : row + 1, :] * vals[j]
                outs[i][k, :, cols] = total
                o_ref[lax.bitwise_xor(x, i), pl.ds(k * 4 + t, 8, stride=8), :] = weighted(out, total)


def pair_kernel(cs_ref, x_ref, tot_ref, pre_ref):
    upper = (lax.axis_index("gz") % 2) == 1
    near, far = jnp.where(upper, 1.0, STEP_Z), jnp.where(upper, STEP_Z, 1.0)
    tot_ref[0] = near * cs_ref[0] + far * x_ref[0]
    tot_ref[1] = far * cs_ref[1] + near * x_ref[1]
    pre_ref[0] = jnp.where(upper, x_ref[0], 0.0)
    pre_ref[1] = jnp.where(upper, 0.0, x_ref[1])


def quad_kernel(tot_ref, x_ref, pre_ref, send_ref, pre2_ref):
    e = lax.axis_index("gz")
    upper = ((e // 2) % 2) == 1
    odd = (e % 2) == 1
    two = STEP_Z * STEP_Z
    near, far = jnp.where(upper, 1.0, two), jnp.where(upper, two, 1.0)
    top = (e // 4) == 1
    send_ref[...] = jnp.where(top, far * tot_ref[1] + near * x_ref[1], near * tot_ref[0] + far * x_ref[0])
    low = jnp.where(odd, STEP_Z, 1.0)
    high = jnp.where(odd, 1.0, STEP_Z)
    pre2_ref[0] = pre_ref[0] + jnp.where(upper, low * x_ref[0], 0.0)
    pre2_ref[1] = pre_ref[1] + jnp.where(upper, 0.0, high * x_ref[1])


def own_kernel(p0_ref, p1_ref, p2_ref, p3_ref, sums_ref, dz_ref, p4):
    x = lax.rem(lax.axis_index("gy"), GX)
    for i, ref in enumerate((p0_ref, p1_ref, p2_ref, p3_ref)):
        p4[lax.bitwise_xor(x, i)] = ref[...]
    own = weights(sums_ref, 0)
    for k in range(2):
        for t in range(16):
            p = p4[t // 4, k, :, (t % 4) * 128 : (t % 4 + 1) * 128]
            dz_ref[k, :, t * 128 : (t + 1) * 128] = weighted(own, p)


def near_kernel(loc_ref, dz_ref, tv_ref, o_ref):
    for l in range(LY):
        for t in range(NX // 128):
            cols = slice(t * 128, (t + 1) * 128)
            o_ref[l, :, cols] = (loc_ref[l, :, cols] + tv_ref[l : l + 1, :] * dz_ref[0, :, cols]
                                 + tv_ref[16 + l : 17 + l, :] * dz_ref[1, :, cols])


def final_kernel(near_ref, pre_ref, x_ref, r_ref, sums_ref, o_hbm, cl, ch, o_ref, sems):
    d, e = lax.axis_index("gy"), lax.axis_index("gz")
    low_rows, high_rows = [], []
    for q in range(GX):
        lo = jnp.zeros((8, 128), F32)
        hi = jnp.zeros((8, 128), F32)
        for p in range(DZ):
            part = r_ref[q * DZ + p]
            lo += jnp.where(p < e, part, 0.0)
            hi += jnp.where(p > e, part, 0.0)
        low_rows.append(lo)
        high_rows.append(hi)
    top = (e // 4) == 1
    at = lax.rem(e, 4)
    power = lambda k: jnp.where(k == 0, 1.0, jnp.where(k == 1, STEP_Z, jnp.where(k == 2, STEP_Z**2, STEP_Z**3)))
    up = jnp.where(top, power(at), 0.0)
    down = jnp.where(top, 0.0, power(3 - at))
    tg, tm = sums_ref[d], sums_ref[DY + e]
    ga = jnp.broadcast_to(tg[:, 0:1], (16, 128))
    gb = jnp.broadcast_to(tg[:, 1:2], (16, 128))
    for t in range(NX // 128):
        cols = slice(t * 128, (t + 1) * 128)
        q, i = t // 4, t % 4
        lo, hi = low_rows[q], high_rows[q]
        cl[:, cols] = (pre_ref[0, :, cols] + up * x_ref[:, cols]) + (ga * lo[i : i + 1] + gb * lo[4 + i : 5 + i])
        ch[:, cols] = (pre_ref[1, :, cols] + down * x_ref[:, cols]) + (ga * hi[i : i + 1] + gb * hi[4 + i : 5 + i])
    hl = jnp.broadcast_to(tm[:8, 8:9], (8, 128))
    hh = jnp.broadcast_to(tm[:8, 9:10], (8, 128))
    stores = []
    for l in range(LY):
        for t in range(NX // 128):
            cols = slice(t * 128, (t + 1) * 128)
            o_ref[l, :, cols] = near_ref[l, :, cols] + (hl * cl[l : l + 1, cols] + hh * ch[l : l + 1, cols])
        if l % 4 == 3:
            i = l // 4
            stores += start((o_ref.at[pl.ds(l - 3, 4)], o_hbm.at[pl.ds(l - 3, 4)], sems.at[i]))
    for store in stores:
        store.wait()


VMEM = pl.BlockSpec(memory_space=pltpu.VMEM)
HBM = pl.BlockSpec(memory_space=pltpu.HBM)
FULL, QUARTER, SUMS_Z = (LY, LZ, NX), (2, LZ, Q), (2, LY, NX)


def call(kernel, outs, ins, out_specs, scratch, mib, name, cost=None):
    if cost is not None:
        cost = pl.CostEstimate(flops=cost[0], bytes_accessed=cost[1], transcendentals=0)
    return pl.pallas_call(
        kernel,
        out_shape=tuple(o if isinstance(o, jax.ShapeDtypeStruct) else jax.ShapeDtypeStruct(o, F32) for o in outs),
        in_specs=ins,
        out_specs=tuple(out_specs),
        scratch_shapes=scratch,
        compiler_params=pltpu.CompilerParams(vmem_limit_bytes=mib * 2**20),
        cost_estimate=cost,
        name=name,
    )


def pairs(count, odd):
    out = []
    for i in range(count):
        j = i + 1 if (i % 2 == 1) == odd else i - 1
        if 0 <= j < count:
            out.append((i, j))
    return out


def across(value, axis, count, bit):
    return lax.ppermute(value, axis, [(i, i ^ bit) for i in range(count)])


tie = lambda *values: lax.optimization_barrier(values)
SMALL = (10**5, 5 * 10**5)
LAYER = [[(z * GX + x) * DZ + e for x in range(GX) for e in range(DZ)] for z in range(GZ)]
COLUMN = [[z * GX + x for z in range(GZ)] for x in range(GX)]


def on_device(temp, vel):
    dma = pltpu.SemaphoreType.DMA
    bf = lambda *shape: jax.ShapeDtypeStruct(shape, BF16)
    y1, y2, z1, z2 = call(
        faces_kernel, [(LZ, NX), (LZ, NX), (LY, NX), (LY, NX)], [VMEM], [VMEM] * 4, [], 4, "faces"
    )(temp)
    y1 = lax.ppermute(y1, "gy", pairs(DY, False))
    y2 = lax.ppermute(y2, "gy", pairs(DY, True))
    z1 = lax.ppermute(z1, "gz", pairs(DZ, False))
    z2 = lax.ppermute(z2, "gz", pairs(DZ, True))
    f, mf, ml, wx, tv = call(
        inner_kernel,
        [FULL, bf(ROWS + 32, 256), bf(ROWS + 32, 128), bf(2, XB, XB), (128, 128)],
        [VMEM] * 3,
        [VMEM] * 5,
        [],
        16,
        "inner",
        (10**7, 8 * 10**6),
    )(temp, vel, SCAL)
    f, *mine = call(
        source_kernel,
        [FULL] + [QUARTER] * 4,
        [VMEM] * 8,
        [VMEM] * 5,
        [
            pltpu.VMEM((NB, 16, XB), BF16),
            pltpu.VMEM((NB, 16, XB), BF16),
            pltpu.VMEM((NB, 16, XB), F32),
            pltpu.VMEM((GX, 2, LZ, Q), F32),
        ],
        16,
        "source",
    )(f, vel, y1, y2, z1, z2, wx, tv)
    sets = [mine[0]] + [across(mine[i], "gy", DY, i) for i in (1, 2, 3)]
    loc, c = call(
        local_kernel,
        [FULL, SUMS_Z],
        [VMEM] * 4,
        [VMEM] * 2,
        [
            pltpu.VMEM((NB, ROWS, XB), BF16),
            pltpu.VMEM((NB, ROWS, XB), BF16),
            pltpu.VMEM((NB, ROWS, XB), F32),
            pltpu.VMEM((2 * ROWS, NX), BF16),
        ],
        16,
        "local",
        (2 * 10**9, 8 * 10**6),
    )(f, wx, mf, ml)
    c, sets[1] = tie(c, sets[1])
    x1 = across(c, "gz", DZ, 1)
    tots = call(group_kernel, [(GZ, LZ, Q)], [VMEM] * 5, [VMEM], [], 4, "group", SMALL)(*sets, tv)[0]
    r1 = lax.all_to_all(tots, "gy", 0, 0, axis_index_groups=COLUMN)
    tot, pre = call(pair_kernel, [SUMS_Z] * 2, [VMEM] * 2, [VMEM] * 2, [], 4, "pair", SMALL)(c, x1)
    x2 = across(tot, "gz", DZ, 2)
    r1, tot, pre = tie(r1, tot, pre)
    *mine, s = call(
        spread_kernel, [QUARTER] * 4 + [(GX, 64, 128)], [VMEM] * 7, [VMEM] * 5, [], 4, "spread", SMALL
    )(*sets, r1, tv, SUMS)
    r3 = lax.all_to_all(s.reshape(GX * DZ, 8, 128), ("gy", "gz"), 0, 0, axis_index_groups=LAYER)
    sets = [mine[0]] + [across(mine[i], "gy", DY, i) for i in (1, 2, 3)]
    x2, sets[0] = tie(x2, sets[0])
    send, pre = call(quad_kernel, [(LY, NX), SUMS_Z], [VMEM] * 3, [VMEM] * 2, [], 4, "quad", SMALL)(tot, x2, pre)
    x3 = across(send, "gz", DZ, 4)
    dz = call(
        own_kernel, [(2, LZ, NX)], [VMEM] * 5, [VMEM], [pltpu.VMEM((GX, 2, LZ, Q), F32)], 8, "own", SMALL
    )(*sets, SUMS)[0]
    near = call(near_kernel, [FULL], [VMEM] * 3, [VMEM], [], 8, "near", (10**6, 2 * 10**6))(loc, dz, tv)[0]
    return call(
        final_kernel,
        [FULL],
        [VMEM] * 5,
        [HBM],
        [pltpu.VMEM((LY, NX), F32), pltpu.VMEM((LY, NX), F32), pltpu.VMEM(FULL, F32), dma((4,))],
        16,
        "final",
    )(near, pre, x3, r3, SUMS)[0]


def solution(mesh):
    return jax.shard_map(
        on_device,
        mesh=mesh,
        in_specs=(P("gy", "gz", None), P(None, "gy", "gz", None)),
        out_specs=P("gy", "gz", None),
        check_vma=False,
    )
```

```python
import jax
import jax.numpy as jnp
import numpy as np
from jax import lax
from jax.experimental import pallas as pl
from jax.experimental.pallas import tpu as pltpu
from jax.sharding import PartitionSpec as P

NX, NY, NZ = 2048, 512, 64
RX, RY, RZ = 1, 768, 192
DY, DZ = 32, 8
GX, GZ = 4, 8
Q = NX // GX
LY, LZ = NY // DY, NZ // DZ
XB = 256
NB = NX // XB
KAPPA = 0.15
F32, BF16 = jnp.float32, jnp.bfloat16


def decay(ratio):
    half = 0.5 / ratio
    return 1.0 + half - np.sqrt(half * (2.0 + half))


QX, QY, QZ = decay(RX), decay(RY), decay(RZ)


STEP_Z = float(QZ**LZ)
ROWS = LY * LZ


def halves(value):
    high = value.astype(BF16)
    return high, (value - high.astype(F32)).astype(BF16)


def mm(a, b):
    return jnp.dot(a, b, preferred_element_type=F32)


def start(*pairs_and_sem):
    copies = [pltpu.make_async_copy(*p) for p in pairs_and_sem]
    for c in copies:
        c.start()
    return copies


def power(q, k):
    return jnp.exp2(k * float(np.log2(q)))


def solve_x(high, low, wx_ref, g, put):
    lines = high.shape[1]
    wh, wl = wx_ref[0], wx_ref[1]
    xh = high[...].reshape(NB * lines, XB)
    xl = low[...].reshape(NB * lines, XB)
    g[...] = (mm(xh, wh) + (mm(xh, wl) + mm(xl, wh))).reshape(NB, lines, XB)
    lane = lax.broadcasted_iota(jnp.int32, (8, 128), 1).astype(F32)
    left, right = power(QX, lane + 1.0)[0:1], power(QX, 128.0 - lane)[0:1]
    for b in range(NB):
        before = g[b - 1, :, XB - 1 :] if b > 0 else g[0, :, :1] * (-QX)
        after = g[b + 1, :, :1] if b < NB - 1 else g[NB - 1, :, XB - 1 :] * (-QX)
        put(2 * b, g[b, :, :128] + before * left)
        put(2 * b + 1, g[b, :, 128:] + after * right)


def faces_kernel(t_ref, y1_ref, y2_ref, z1_ref, z2_ref):
    d, e = lax.axis_index("gy"), lax.axis_index("gz")
    odd_y, odd_z = (d % 2) == 1, (e % 2) == 1
    first, last = t_ref[0], t_ref[LY - 1]
    y1_ref[...] = jnp.where(odd_y, first, last)
    y2_ref[...] = jnp.where(odd_y, last, first)
    for y in range(LY):
        bottom, top = t_ref[y, 0:1, :], t_ref[y, LZ - 1 : LZ, :]
        z1_ref[y : y + 1, :] = jnp.where(odd_z, bottom, top)
        z2_ref[y : y + 1, :] = jnp.where(odd_z, top, bottom)


def inner_kernel(t_ref, v_ref, f_ref, mf_ref, ml_ref, wx_ref, tv_ref, tz_ref):
    d, e = lax.axis_index("gy"), lax.axis_index("gz")
    zi = lax.broadcasted_iota(jnp.int32, (LZ, NX), 0)
    xi = lax.broadcasted_iota(jnp.int32, (LZ, NX), 1)
    nothing = jnp.zeros((LZ, NX), F32)
    for y in range(LY):
        t = t_ref[y]
        north = t_ref[y + 1] if y < LY - 1 else nothing
        south = t_ref[y - 1] if y > 0 else nothing
        ceil = jnp.where(zi == LZ - 1, 0.0, pltpu.roll(t, LZ - 1, 0))
        floor = jnp.where(zi == 0, 0.0, pltpu.roll(t, 1, 0))
        east = jnp.where(xi == NX - 1, 0.0, pltpu.roll(t, NX - 1, 1))
        west = jnp.where(xi == 0, 0.0, pltpu.roll(t, 1, 1))
        lap = ((east + west) + (north + south)) + (ceil + floor) - 6.0 * t
        adv = (v_ref[0, y].astype(F32) * (east - west) + v_ref[1, y].astype(F32) * (north - south)
               + v_ref[2, y].astype(F32) * (ceil - floor))
        f_ref[y] = t + KAPPA * lap - 0.5 * adv
    i = lax.broadcasted_iota(jnp.int32, (XB, XB), 0)
    j = lax.broadcasted_iota(jnp.int32, (XB, XB), 1)
    w = power(QX, (jnp.abs(i - j) + 1).astype(F32)) * (1.0 / (RX * (1 - QX * QX)))
    wx_ref[0], wx_ref[1] = halves(w)
    lane = lax.broadcasted_iota(jnp.int32, (16, 128), 1)
    sub = lax.broadcasted_iota(jnp.int32, (16, 128), 0)

    def block(q, ratio, count, first, own, other):
        small = (jnp.minimum(own, other) + first + 1).astype(F32)
        large = (count - first - jnp.maximum(own, other)).astype(F32)
        gap = (jnp.abs(own - other) + 1).astype(F32)
        return (power(q, gap) * (1.0 - power(q, 2.0 * small)) * (1.0 - power(q, 2.0 * large))
                * (1.0 / (ratio * (1 - q * q) * (1 - q ** (2.0 * count + 2)))))

    my = block(QY, RY, NY, d * LY, sub, lane // LZ)
    w8 = (lane % LZ)[:8]
    mz = block(QZ, RZ, NZ, e * LZ, sub[:8], w8)
    up = power(QZ, (LZ - 1 - w8).astype(F32)) * (1.0 - power(QZ, 2.0 * (w8 + e * LZ + 1).astype(F32)))
    down = power(QZ, w8.astype(F32)) * (1.0 - power(QZ, 2.0 * (NZ - e * LZ - w8).astype(F32)))
    wide, x, z = sub.astype(F32), lax.rem(d, GX), d // GX
    at = (sub + d * LY).astype(F32)
    low, high = 1.0 - power(QY, 2.0 * at + 2.0), 1.0 - power(QY, 2.0 * (NY - at))
    scale = 1.0 / (RY * (1 - QY * QY) * (1 - QY ** (2.0 * NY + 2)))
    tv_ref[0:16] = power(QY, wide + 2.0) * high * scale
    tv_ref[16:32] = power(QY, LY + 1.0 - wide) * low * scale
    tv_ref[32:48] = power(QY, LY - 1.0 - wide) * low
    tv_ref[48:64] = power(QY, wide) * high
    s8 = sub[:8]
    xi = (s8 & (GX - 1)) ^ x
    tv_ref[64:72] = power(QY, (LY * jnp.where(s8 < GX, GX - 1 - xi, xi)).astype(F32))
    gap = jnp.abs(s8 - z)
    tv_ref[72:80] = jnp.where(gap == 0, 0.0, power(QY, (LY * GX * (gap - 1)).astype(F32)))
    ahead = ((sub >> 2) ^ x) - ((sub & (GX - 1)) ^ x)
    tv_ref[80:96] = jnp.where(ahead > 0, power(QY, (LY * (ahead - 1)).astype(F32)), 0.0)
    tv_ref[96:112] = jnp.where(ahead < 0, power(QY, (LY * (-ahead - 1)).astype(F32)), 0.0)
    tv_ref[112:128] = jnp.zeros((16, 128), F32)
    gap = jnp.abs(s8 - e)
    reach = power(QZ, (LZ * (gap - 1)).astype(F32))
    tz_ref[0:8] = mz
    tz_ref[8:16] = jnp.where(s8 > e, up * reach, jnp.where(s8 < e, down * reach, 0.0))
    wide, at = s8.astype(F32), (s8 + e * LZ).astype(F32)
    scale = 1.0 / (RZ * (1 - QZ * QZ) * (1 - QZ ** (2.0 * NZ + 2)))
    tz_ref[16:24] = power(QZ, wide + 2.0) * (1.0 - power(QZ, 2.0 * (NZ - at))) * scale
    tz_ref[24:32] = power(QZ, LZ + 1.0 - wide) * (1.0 - power(QZ, 2.0 * at + 2.0)) * scale
    for l in range(LY // 2):
        pair = jnp.concatenate([my[2 * l : 2 * l + 1] * mz, my[2 * l + 1 : 2 * l + 2] * mz], axis=0)
        high, low = halves(pair)
        mf_ref[16 * l : 16 * l + 16, :128] = high
        mf_ref[16 * l : 16 * l + 16, 128:] = high
        ml_ref[16 * l : 16 * l + 16] = low
    for k, part in ((0, up), (1, down)):
        high, low = halves(my * part[0:1])
        at = ROWS + 16 * k
        mf_ref[at : at + 16, :128] = high
        mf_ref[at : at + 16, 128:] = high
        ml_ref[at : at + 16] = low


def source_kernel(f0_ref, v_ref, y1_ref, y2_ref, z1_ref, z2_ref, wx_ref, tv_ref,
                  f_ref, own_ref, s1_ref, s2_ref, s3_ref, ah, al, g, a4):
    d, e = lax.axis_index("gy"), lax.axis_index("gz")
    odd_y, odd_z = (d % 2) == 1, (e % 2) == 1
    zi = lax.broadcasted_iota(jnp.int32, (LZ, XB), 0)
    for b in range(NB):
        cols = slice(b * XB, (b + 1) * XB)
        sums = [jnp.zeros((LZ, XB), F32), jnp.zeros((LZ, XB), F32)]
        for y in range(LY):
            f = f0_ref[y, :, cols]
            w = 0.5 * v_ref[2, y, :, cols].astype(F32)
            h1, h2 = z1_ref[y : y + 1, cols], z2_ref[y : y + 1, cols]
            above, below = jnp.where(odd_z, h2, h1), jnp.where(odd_z, h1, h2)
            f += jnp.where(zi == 0, (KAPPA + w) * below, jnp.where(zi == LZ - 1, (KAPPA - w) * above, 0.0))
            if y == 0:
                south = jnp.where(odd_y, y1_ref[:, cols], y2_ref[:, cols])
                f += (KAPPA + 0.5 * v_ref[1, y, :, cols].astype(F32)) * south
            if y == LY - 1:
                north = jnp.where(odd_y, y2_ref[:, cols], y1_ref[:, cols])
                f += (KAPPA - 0.5 * v_ref[1, y, :, cols].astype(F32)) * north
            f_ref[y, :, cols] = f
            for k in range(2):
                c = tv_ref[32 + 16 * k + y : 33 + 16 * k + y, :]
                sums[k] += f * jnp.concatenate([c, c], axis=1)
        high, low = halves(jnp.concatenate(sums, axis=0))
        ah[b] = high
        al[b] = low

    def put(t, part):
        for k in range(2):
            a4[t // 4, k, :, (t % 4) * 128 : (t % 4 + 1) * 128] = part[8 * k : 8 * k + 8]

    solve_x(ah, al, wx_ref, g, put)
    x = lax.rem(d, GX)
    for i, ref in enumerate((own_ref, s1_ref, s2_ref, s3_ref)):
        ref[...] = a4[lax.bitwise_xor(x, i)]


def local_kernel(f_ref, wx_ref, mf_ref, ml_ref, loc_ref, c_ref, fh, fl, g, ghl):
    for b in range(NB):
        high, low = halves(f_ref[:, :, b * XB : (b + 1) * XB].reshape(ROWS, XB))
        fh[b] = high
        fl[b] = low

    def put(t, part):
        high, low = halves(part)
        ghl[:ROWS, t * 128 : (t + 1) * 128] = high
        ghl[ROWS:, t * 128 : (t + 1) * 128] = low

    solve_x(fh, fl, wx_ref, g, put)
    for b in range(NB):
        cols = slice(b * XB, (b + 1) * XB)
        out = mm(mf_ref[...], ghl[:, cols]) + mm(ml_ref[...], ghl[:ROWS, cols])
        loc_ref[:, :, cols] = out[:ROWS].reshape(LY, LZ, XB)
        c_ref[0, :, cols] = out[ROWS : ROWS + 16]
        c_ref[1, :, cols] = out[ROWS + 16 :]


def group_kernel(a_ref, b_ref, c_ref, d_ref, tv_ref, o_ref):
    z = lax.axis_index("gy") // GX
    parts = (a_ref, b_ref, c_ref, d_ref)
    for t in range(Q // 128):
        cols = slice(t * 128, (t + 1) * 128)
        tot = []
        for k in range(2):
            base = 64 + 4 * k
            tot.append(sum(tv_ref[base + i : base + i + 1, :] * parts[i][k, :, cols] for i in range(4)))
        for p in range(GZ):
            o_ref[p, :, cols] = tv_ref[72 + p : 73 + p, :] * jnp.where(p > z, tot[0], tot[1])


def weights(tz_ref, first):
    return [jnp.broadcast_to(tz_ref[first : first + 8, w : w + 1], (8, 128)) for w in range(8)]


def weighted(rows, p):
    total = rows[0] * p[0:1]
    for w in range(1, 8):
        total += rows[w] * p[w : w + 1]
    return total


def spread_kernel(a_ref, b_ref, c_ref, d_ref, r_ref, tv_ref, tz_ref, own_ref, s1_ref, s2_ref, s3_ref, o_ref):
    d = lax.axis_index("gy")
    z, x = d // GX, lax.rem(d, GX)
    out = weights(tz_ref, 8)
    parts = (a_ref, b_ref, c_ref, d_ref)
    outs = (own_ref, s1_ref, s2_ref, s3_ref)
    for t in range(Q // 128):
        cols = slice(t * 128, (t + 1) * 128)
        low = jnp.zeros((8, 128), F32)
        high = jnp.zeros((8, 128), F32)
        for p in range(GZ):
            part = r_ref[p, :, cols]
            low += jnp.where(p < z, part, 0.0)
            high += jnp.where(p > z, part, 0.0)
        for k, group in ((0, low), (1, high)):
            vals = [ref[k, :, cols] for ref in parts]
            for i in range(4):
                at = 68 + i if k == 0 else 64 + i
                total = tv_ref[at : at + 1, :] * group
                for j in range(4):
                    if j != i:
                        row = 80 + 16 * k + 4 * i + j
                        total += tv_ref[row : row + 1, :] * vals[j]
                outs[i][k, :, cols] = total
                o_ref[lax.bitwise_xor(x, i), pl.ds(k * 4 + t, 8, stride=8), :] = weighted(out, total)


def pair_kernel(cs_ref, x_ref, tot_ref, pre_ref):
    upper = (lax.axis_index("gz") % 2) == 1
    near, far = jnp.where(upper, 1.0, STEP_Z), jnp.where(upper, STEP_Z, 1.0)
    tot_ref[0] = near * cs_ref[0] + far * x_ref[0]
    tot_ref[1] = far * cs_ref[1] + near * x_ref[1]
    pre_ref[0] = jnp.where(upper, x_ref[0], 0.0)
    pre_ref[1] = jnp.where(upper, 0.0, x_ref[1])


def quad_kernel(tot_ref, x_ref, pre_ref, send_ref, pre2_ref):
    e = lax.axis_index("gz")
    upper = ((e // 2) % 2) == 1
    odd = (e % 2) == 1
    two = STEP_Z * STEP_Z
    near, far = jnp.where(upper, 1.0, two), jnp.where(upper, two, 1.0)
    top = (e // 4) == 1
    send_ref[...] = jnp.where(top, far * tot_ref[1] + near * x_ref[1], near * tot_ref[0] + far * x_ref[0])
    low = jnp.where(odd, STEP_Z, 1.0)
    high = jnp.where(odd, 1.0, STEP_Z)
    pre2_ref[0] = pre_ref[0] + jnp.where(upper, low * x_ref[0], 0.0)
    pre2_ref[1] = pre_ref[1] + jnp.where(upper, 0.0, high * x_ref[1])


def own_kernel(p0_ref, p1_ref, p2_ref, p3_ref, tz_ref, dz_ref, p4):
    x = lax.rem(lax.axis_index("gy"), GX)
    for i, ref in enumerate((p0_ref, p1_ref, p2_ref, p3_ref)):
        p4[lax.bitwise_xor(x, i)] = ref[...]
    own = weights(tz_ref, 0)
    for k in range(2):
        for t in range(16):
            p = p4[t // 4, k, :, (t % 4) * 128 : (t % 4 + 1) * 128]
            dz_ref[k, :, t * 128 : (t + 1) * 128] = weighted(own, p)


def near_kernel(loc_ref, dz_ref, tv_ref, o_ref):
    for l in range(LY):
        for t in range(NX // 128):
            cols = slice(t * 128, (t + 1) * 128)
            o_ref[l, :, cols] = (loc_ref[l, :, cols] + tv_ref[l : l + 1, :] * dz_ref[0, :, cols]
                                 + tv_ref[16 + l : 17 + l, :] * dz_ref[1, :, cols])


def final_kernel(near_ref, pre_ref, x_ref, r_ref, tz_ref, tv_ref, o_hbm, cl, ch, o_ref, sems):
    e = lax.axis_index("gz")
    low_rows, high_rows = [], []
    for q in range(GX):
        lo = jnp.zeros((8, 128), F32)
        hi = jnp.zeros((8, 128), F32)
        for p in range(DZ):
            part = r_ref[q * DZ + p]
            lo += jnp.where(p < e, part, 0.0)
            hi += jnp.where(p > e, part, 0.0)
        low_rows.append(lo)
        high_rows.append(hi)
    top = (e // 4) == 1
    at = lax.rem(e, 4)
    power = lambda k: jnp.where(k == 0, 1.0, jnp.where(k == 1, STEP_Z, jnp.where(k == 2, STEP_Z**2, STEP_Z**3)))
    up = jnp.where(top, power(at), 0.0)
    down = jnp.where(top, 0.0, power(3 - at))
    ga, gb = tv_ref[0:16], tv_ref[16:32]
    for t in range(NX // 128):
        cols = slice(t * 128, (t + 1) * 128)
        q, i = t // 4, t % 4
        lo, hi = low_rows[q], high_rows[q]
        cl[:, cols] = (pre_ref[0, :, cols] + up * x_ref[:, cols]) + (ga * lo[i : i + 1] + gb * lo[4 + i : 5 + i])
        ch[:, cols] = (pre_ref[1, :, cols] + down * x_ref[:, cols]) + (ga * hi[i : i + 1] + gb * hi[4 + i : 5 + i])
    hl, hh = tz_ref[16:24], tz_ref[24:32]
    stores = []
    for l in range(LY):
        for t in range(NX // 128):
            cols = slice(t * 128, (t + 1) * 128)
            o_ref[l, :, cols] = near_ref[l, :, cols] + (hl * cl[l : l + 1, cols] + hh * ch[l : l + 1, cols])
        if l % 4 == 3:
            i = l // 4
            stores += start((o_ref.at[pl.ds(l - 3, 4)], o_hbm.at[pl.ds(l - 3, 4)], sems.at[i]))
    for store in stores:
        store.wait()


VMEM = pl.BlockSpec(memory_space=pltpu.VMEM)
HBM = pl.BlockSpec(memory_space=pltpu.HBM)
FULL, QUARTER, SUMS_Z = (LY, LZ, NX), (2, LZ, Q), (2, LY, NX)


def call(kernel, outs, ins, out_specs, scratch, mib, name, cost=None):
    if cost is not None:
        cost = pl.CostEstimate(flops=cost[0], bytes_accessed=cost[1], transcendentals=0)
    return pl.pallas_call(
        kernel,
        out_shape=tuple(o if isinstance(o, jax.ShapeDtypeStruct) else jax.ShapeDtypeStruct(o, F32) for o in outs),
        in_specs=ins,
        out_specs=tuple(out_specs),
        scratch_shapes=scratch,
        compiler_params=pltpu.CompilerParams(vmem_limit_bytes=mib * 2**20),
        cost_estimate=cost,
        name=name,
    )


def pairs(count, odd):
    out = []
    for i in range(count):
        j = i + 1 if (i % 2 == 1) == odd else i - 1
        if 0 <= j < count:
            out.append((i, j))
    return out


def across(value, axis, count, bit):
    return lax.ppermute(value, axis, [(i, i ^ bit) for i in range(count)])


tie = lambda *values: lax.optimization_barrier(values)
SMALL = (10**5, 5 * 10**5)
LAYER = [[(z * GX + x) * DZ + e for x in range(GX) for e in range(DZ)] for z in range(GZ)]
COLUMN = [[z * GX + x for z in range(GZ)] for x in range(GX)]


def on_device(temp, vel):
    dma = pltpu.SemaphoreType.DMA
    bf = lambda *shape: jax.ShapeDtypeStruct(shape, BF16)
    y1, y2, z1, z2 = call(
        faces_kernel, [(LZ, NX), (LZ, NX), (LY, NX), (LY, NX)], [VMEM], [VMEM] * 4, [], 4, "faces"
    )(temp)
    y1 = lax.ppermute(y1, "gy", pairs(DY, False))
    y2 = lax.ppermute(y2, "gy", pairs(DY, True))
    z1 = lax.ppermute(z1, "gz", pairs(DZ, False))
    z2 = lax.ppermute(z2, "gz", pairs(DZ, True))
    f, mf, ml, wx, tv, tz = call(
        inner_kernel,
        [FULL, bf(ROWS + 32, 256), bf(ROWS + 32, 128), bf(2, XB, XB), (128, 128), (32, 128)],
        [VMEM] * 2,
        [VMEM] * 6,
        [],
        16,
        "inner",
        (10**7, 8 * 10**6),
    )(temp, vel)
    f, *mine = call(
        source_kernel,
        [FULL] + [QUARTER] * 4,
        [VMEM] * 8,
        [VMEM] * 5,
        [
            pltpu.VMEM((NB, 16, XB), BF16),
            pltpu.VMEM((NB, 16, XB), BF16),
            pltpu.VMEM((NB, 16, XB), F32),
            pltpu.VMEM((GX, 2, LZ, Q), F32),
        ],
        16,
        "source",
    )(f, vel, y1, y2, z1, z2, wx, tv)
    sets = [mine[0]] + [across(mine[i], "gy", DY, i) for i in (1, 2, 3)]
    loc, c = call(
        local_kernel,
        [FULL, SUMS_Z],
        [VMEM] * 4,
        [VMEM] * 2,
        [
            pltpu.VMEM((NB, ROWS, XB), BF16),
            pltpu.VMEM((NB, ROWS, XB), BF16),
            pltpu.VMEM((NB, ROWS, XB), F32),
            pltpu.VMEM((2 * ROWS, NX), BF16),
        ],
        16,
        "local",
        (2 * 10**9, 8 * 10**6),
    )(f, wx, mf, ml)
    c, sets[1] = tie(c, sets[1])
    x1 = across(c, "gz", DZ, 1)
    tots = call(group_kernel, [(GZ, LZ, Q)], [VMEM] * 5, [VMEM], [], 4, "group", SMALL)(*sets, tv)[0]
    r1 = lax.all_to_all(tots, "gy", 0, 0, axis_index_groups=COLUMN)
    tot, pre = call(pair_kernel, [SUMS_Z] * 2, [VMEM] * 2, [VMEM] * 2, [], 4, "pair", SMALL)(c, x1)
    x2 = across(tot, "gz", DZ, 2)
    r1, tot, pre = tie(r1, tot, pre)
    *mine, s = call(
        spread_kernel, [QUARTER] * 4 + [(GX, 64, 128)], [VMEM] * 7, [VMEM] * 5, [], 4, "spread", SMALL
    )(*sets, r1, tv, tz)
    r3 = lax.all_to_all(s.reshape(GX * DZ, 8, 128), ("gy", "gz"), 0, 0, axis_index_groups=LAYER)
    sets = [mine[0]] + [across(mine[i], "gy", DY, i) for i in (1, 2, 3)]
    x2, sets[0] = tie(x2, sets[0])
    send, pre = call(quad_kernel, [(LY, NX), SUMS_Z], [VMEM] * 3, [VMEM] * 2, [], 4, "quad", SMALL)(tot, x2, pre)
    x3 = across(send, "gz", DZ, 4)
    dz = call(
        own_kernel, [(2, LZ, NX)], [VMEM] * 5, [VMEM], [pltpu.VMEM((GX, 2, LZ, Q), F32)], 8, "own", SMALL
    )(*sets, tz)[0]
    near = call(near_kernel, [FULL], [VMEM] * 3, [VMEM], [], 8, "near", (10**6, 2 * 10**6))(loc, dz, tv)[0]
    return call(
        final_kernel,
        [FULL],
        [VMEM] * 6,
        [HBM],
        [pltpu.VMEM((LY, NX), F32), pltpu.VMEM((LY, NX), F32), pltpu.VMEM(FULL, F32), dma((4,))],
        16,
        "final",
    )(near, pre, x3, r3, tz, tv)[0]


def solution(mesh):
    return jax.shard_map(
        on_device,
        mesh=mesh,
        in_specs=(P("gy", "gz", None), P(None, "gy", "gz", None)),
        out_specs=P("gy", "gz", None),
        check_vma=False,
    )
```

```python
import jax
import jax.numpy as jnp
import numpy as np
from jax import lax
from jax.experimental import pallas as pl
from jax.experimental.pallas import tpu as pltpu
from jax.sharding import PartitionSpec as P

NX, NY, NZ = 2048, 512, 64
RX, RY, RZ = 1, 768, 192
DY, DZ = 32, 8
GX, GZ = 4, 8
Q = NX // GX
LY, LZ = NY // DY, NZ // DZ
XB = 256
NB = NX // XB
KAPPA = 0.15
F32, BF16 = jnp.float32, jnp.bfloat16


def decay(ratio):
    half = 0.5 / ratio
    return 1.0 + half - np.sqrt(half * (2.0 + half))


QX, QY, QZ = decay(RX), decay(RY), decay(RZ)


STEP_Z = float(QZ**LZ)
ROWS = LY * LZ


def halves(value):
    high = value.astype(BF16)
    return high, (value - high.astype(F32)).astype(BF16)


def mm(a, b):
    return jnp.dot(a, b, preferred_element_type=F32)


def start(*pairs_and_sem):
    copies = [pltpu.make_async_copy(*p) for p in pairs_and_sem]
    for c in copies:
        c.start()
    return copies


def power(q, k):
    return jnp.exp2(k * float(np.log2(q)))


def solve_x(high, low, wx_ref, g, put):
    lines = high.shape[1]
    wh, wl = wx_ref[0], wx_ref[1]
    xh = high[...].reshape(NB * lines, XB)
    xl = low[...].reshape(NB * lines, XB)
    g[...] = (mm(xh, wh) + (mm(xh, wl) + mm(xl, wh))).reshape(NB, lines, XB)
    lane = lax.broadcasted_iota(jnp.int32, (8, 128), 1).astype(F32)
    left, right = power(QX, lane + 1.0)[0:1], power(QX, 128.0 - lane)[0:1]
    for b in range(NB):
        before = g[b - 1, :, XB - 1 :] if b > 0 else g[0, :, :1] * (-QX)
        after = g[b + 1, :, :1] if b < NB - 1 else g[NB - 1, :, XB - 1 :] * (-QX)
        put(2 * b, g[b, :, :128] + before * left)
        put(2 * b + 1, g[b, :, 128:] + after * right)


def faces_kernel(t_hbm, y1_ref, y2_ref, z1_ref, z2_ref, t_ref, sems):
    d, e = lax.axis_index("gy"), lax.axis_index("gz")
    loads = start(*((t_hbm.at[pl.ds(4 * i, 4)], t_ref.at[pl.ds(4 * i, 4)], sems.at[i]) for i in range(LY // 4)))
    for load in loads:
        load.wait()
    odd_y, odd_z = (d % 2) == 1, (e % 2) == 1
    first, last = t_ref[0], t_ref[LY - 1]
    y1_ref[...] = jnp.where(odd_y, first, last)
    y2_ref[...] = jnp.where(odd_y, last, first)
    for y in range(LY):
        bottom, top = t_ref[y, 0:1, :], t_ref[y, LZ - 1 : LZ, :]
        z1_ref[y : y + 1, :] = jnp.where(odd_z, bottom, top)
        z2_ref[y : y + 1, :] = jnp.where(odd_z, top, bottom)


def inner_kernel(t_ref, v_ref, f_ref, mf_ref, ml_ref, wx_ref, tv_ref, tz_ref):
    d, e = lax.axis_index("gy"), lax.axis_index("gz")
    zi = lax.broadcasted_iota(jnp.int32, (LZ, NX), 0)
    xi = lax.broadcasted_iota(jnp.int32, (LZ, NX), 1)
    nothing = jnp.zeros((LZ, NX), F32)
    for y in range(LY):
        t = t_ref[y]
        north = t_ref[y + 1] if y < LY - 1 else nothing
        south = t_ref[y - 1] if y > 0 else nothing
        ceil = jnp.where(zi == LZ - 1, 0.0, pltpu.roll(t, LZ - 1, 0))
        floor = jnp.where(zi == 0, 0.0, pltpu.roll(t, 1, 0))
        east = jnp.where(xi == NX - 1, 0.0, pltpu.roll(t, NX - 1, 1))
        west = jnp.where(xi == 0, 0.0, pltpu.roll(t, 1, 1))
        lap = ((east + west) + (north + south)) + (ceil + floor) - 6.0 * t
        adv = (v_ref[0, y].astype(F32) * (east - west) + v_ref[1, y].astype(F32) * (north - south)
               + v_ref[2, y].astype(F32) * (ceil - floor))
        f_ref[y] = t + KAPPA * lap - 0.5 * adv
    i = lax.broadcasted_iota(jnp.int32, (XB, XB), 0)
    j = lax.broadcasted_iota(jnp.int32, (XB, XB), 1)
    w = power(QX, (jnp.abs(i - j) + 1).astype(F32)) * (1.0 / (RX * (1 - QX * QX)))
    wx_ref[0], wx_ref[1] = halves(w)
    lane = lax.broadcasted_iota(jnp.int32, (16, 128), 1)
    sub = lax.broadcasted_iota(jnp.int32, (16, 128), 0)

    def block(q, ratio, count, first, own, other):
        small = (jnp.minimum(own, other) + first + 1).astype(F32)
        large = (count - first - jnp.maximum(own, other)).astype(F32)
        gap = (jnp.abs(own - other) + 1).astype(F32)
        return (power(q, gap) * (1.0 - power(q, 2.0 * small)) * (1.0 - power(q, 2.0 * large))
                * (1.0 / (ratio * (1 - q * q) * (1 - q ** (2.0 * count + 2)))))

    my = block(QY, RY, NY, d * LY, sub, lane // LZ)
    w8 = (lane % LZ)[:8]
    mz = block(QZ, RZ, NZ, e * LZ, sub[:8], w8)
    up = power(QZ, (LZ - 1 - w8).astype(F32)) * (1.0 - power(QZ, 2.0 * (w8 + e * LZ + 1).astype(F32)))
    down = power(QZ, w8.astype(F32)) * (1.0 - power(QZ, 2.0 * (NZ - e * LZ - w8).astype(F32)))
    wide, x, z = sub.astype(F32), lax.rem(d, GX), d // GX
    at = (sub + d * LY).astype(F32)
    low, high = 1.0 - power(QY, 2.0 * at + 2.0), 1.0 - power(QY, 2.0 * (NY - at))
    scale = 1.0 / (RY * (1 - QY * QY) * (1 - QY ** (2.0 * NY + 2)))
    tv_ref[0:16] = power(QY, wide + 2.0) * high * scale
    tv_ref[16:32] = power(QY, LY + 1.0 - wide) * low * scale
    tv_ref[32:48] = power(QY, LY - 1.0 - wide) * low
    tv_ref[48:64] = power(QY, wide) * high
    s8 = sub[:8]
    xi = (s8 & (GX - 1)) ^ x
    tv_ref[64:72] = power(QY, (LY * jnp.where(s8 < GX, GX - 1 - xi, xi)).astype(F32))
    gap = jnp.abs(s8 - z)
    tv_ref[72:80] = jnp.where(gap == 0, 0.0, power(QY, (LY * GX * (gap - 1)).astype(F32)))
    ahead = ((sub >> 2) ^ x) - ((sub & (GX - 1)) ^ x)
    tv_ref[80:96] = jnp.where(ahead > 0, power(QY, (LY * (ahead - 1)).astype(F32)), 0.0)
    tv_ref[96:112] = jnp.where(ahead < 0, power(QY, (LY * (-ahead - 1)).astype(F32)), 0.0)
    tv_ref[112:128] = jnp.zeros((16, 128), F32)
    gap = jnp.abs(s8 - e)
    reach = power(QZ, (LZ * (gap - 1)).astype(F32))
    tz_ref[0:8] = mz
    tz_ref[8:16] = jnp.where(s8 > e, up * reach, jnp.where(s8 < e, down * reach, 0.0))
    wide, at = s8.astype(F32), (s8 + e * LZ).astype(F32)
    scale = 1.0 / (RZ * (1 - QZ * QZ) * (1 - QZ ** (2.0 * NZ + 2)))
    tz_ref[16:24] = power(QZ, wide + 2.0) * (1.0 - power(QZ, 2.0 * (NZ - at))) * scale
    tz_ref[24:32] = power(QZ, LZ + 1.0 - wide) * (1.0 - power(QZ, 2.0 * at + 2.0)) * scale
    for l in range(LY // 2):
        pair = jnp.concatenate([my[2 * l : 2 * l + 1] * mz, my[2 * l + 1 : 2 * l + 2] * mz], axis=0)
        high, low = halves(pair)
        mf_ref[16 * l : 16 * l + 16, :128] = high
        mf_ref[16 * l : 16 * l + 16, 128:] = high
        ml_ref[16 * l : 16 * l + 16] = low
    for k, part in ((0, up), (1, down)):
        high, low = halves(my * part[0:1])
        at = ROWS + 16 * k
        mf_ref[at : at + 16, :128] = high
        mf_ref[at : at + 16, 128:] = high
        ml_ref[at : at + 16] = low


def source_kernel(f0_ref, v_ref, y1_ref, y2_ref, z1_ref, z2_ref, wx_ref, tv_ref,
                  f_ref, own_ref, s1_ref, s2_ref, s3_ref, ah, al, g, a4):
    d, e = lax.axis_index("gy"), lax.axis_index("gz")
    odd_y, odd_z = (d % 2) == 1, (e % 2) == 1
    zi = lax.broadcasted_iota(jnp.int32, (LZ, XB), 0)
    for b in range(NB):
        cols = slice(b * XB, (b + 1) * XB)
        sums = [jnp.zeros((LZ, XB), F32), jnp.zeros((LZ, XB), F32)]
        for y in range(LY):
            f = f0_ref[y, :, cols]
            w = 0.5 * v_ref[2, y, :, cols].astype(F32)
            h1, h2 = z1_ref[y : y + 1, cols], z2_ref[y : y + 1, cols]
            above, below = jnp.where(odd_z, h2, h1), jnp.where(odd_z, h1, h2)
            f += jnp.where(zi == 0, (KAPPA + w) * below, jnp.where(zi == LZ - 1, (KAPPA - w) * above, 0.0))
            if y == 0:
                south = jnp.where(odd_y, y1_ref[:, cols], y2_ref[:, cols])
                f += (KAPPA + 0.5 * v_ref[1, y, :, cols].astype(F32)) * south
            if y == LY - 1:
                north = jnp.where(odd_y, y2_ref[:, cols], y1_ref[:, cols])
                f += (KAPPA - 0.5 * v_ref[1, y, :, cols].astype(F32)) * north
            f_ref[y, :, cols] = f
            for k in range(2):
                c = tv_ref[32 + 16 * k + y : 33 + 16 * k + y, :]
                sums[k] += f * jnp.concatenate([c, c], axis=1)
        high, low = halves(jnp.concatenate(sums, axis=0))
        ah[b] = high
        al[b] = low

    def put(t, part):
        for k in range(2):
            a4[t // 4, k, :, (t % 4) * 128 : (t % 4 + 1) * 128] = part[8 * k : 8 * k + 8]

    solve_x(ah, al, wx_ref, g, put)
    x = lax.rem(d, GX)
    for i, ref in enumerate((own_ref, s1_ref, s2_ref, s3_ref)):
        ref[...] = a4[lax.bitwise_xor(x, i)]


def local_kernel(f_ref, wx_ref, mf_ref, ml_ref, loc_ref, c_ref, fh, fl, g, ghl):
    for b in range(NB):
        high, low = halves(f_ref[:, :, b * XB : (b + 1) * XB].reshape(ROWS, XB))
        fh[b] = high
        fl[b] = low

    def put(t, part):
        high, low = halves(part)
        ghl[:ROWS, t * 128 : (t + 1) * 128] = high
        ghl[ROWS:, t * 128 : (t + 1) * 128] = low

    solve_x(fh, fl, wx_ref, g, put)
    for b in range(NB):
        cols = slice(b * XB, (b + 1) * XB)
        out = mm(mf_ref[...], ghl[:, cols]) + mm(ml_ref[...], ghl[:ROWS, cols])
        loc_ref[:, :, cols] = out[:ROWS].reshape(LY, LZ, XB)
        c_ref[0, :, cols] = out[ROWS : ROWS + 16]
        c_ref[1, :, cols] = out[ROWS + 16 :]


def group_kernel(a_ref, b_ref, c_ref, d_ref, tv_ref, o_ref):
    z = lax.axis_index("gy") // GX
    parts = (a_ref, b_ref, c_ref, d_ref)
    for t in range(Q // 128):
        cols = slice(t * 128, (t + 1) * 128)
        tot = []
        for k in range(2):
            base = 64 + 4 * k
            tot.append(sum(tv_ref[base + i : base + i + 1, :] * parts[i][k, :, cols] for i in range(4)))
        for p in range(GZ):
            o_ref[p, :, cols] = tv_ref[72 + p : 73 + p, :] * jnp.where(p > z, tot[0], tot[1])


def weights(tz_ref, first):
    return [jnp.broadcast_to(tz_ref[first : first + 8, w : w + 1], (8, 128)) for w in range(8)]


def weighted(rows, p):
    total = rows[0] * p[0:1]
    for w in range(1, 8):
        total += rows[w] * p[w : w + 1]
    return total


def spread_kernel(a_ref, b_ref, c_ref, d_ref, r_ref, tv_ref, tz_ref, own_ref, s1_ref, s2_ref, s3_ref, o_ref):
    d = lax.axis_index("gy")
    z, x = d // GX, lax.rem(d, GX)
    out = weights(tz_ref, 8)
    parts = (a_ref, b_ref, c_ref, d_ref)
    outs = (own_ref, s1_ref, s2_ref, s3_ref)
    for t in range(Q // 128):
        cols = slice(t * 128, (t + 1) * 128)
        low = jnp.zeros((8, 128), F32)
        high = jnp.zeros((8, 128), F32)
        for p in range(GZ):
            part = r_ref[p, :, cols]
            low += jnp.where(p < z, part, 0.0)
            high += jnp.where(p > z, part, 0.0)
        for k, group in ((0, low), (1, high)):
            vals = [ref[k, :, cols] for ref in parts]
            for i in range(4):
                at = 68 + i if k == 0 else 64 + i
                total = tv_ref[at : at + 1, :] * group
                for j in range(4):
                    if j != i:
                        row = 80 + 16 * k + 4 * i + j
                        total += tv_ref[row : row + 1, :] * vals[j]
                outs[i][k, :, cols] = total
                o_ref[lax.bitwise_xor(x, i), pl.ds(k * 4 + t, 8, stride=8), :] = weighted(out, total)


def pair_kernel(cs_ref, x_ref, tot_ref, pre_ref):
    upper = (lax.axis_index("gz") % 2) == 1
    near, far = jnp.where(upper, 1.0, STEP_Z), jnp.where(upper, STEP_Z, 1.0)
    tot_ref[0] = near * cs_ref[0] + far * x_ref[0]
    tot_ref[1] = far * cs_ref[1] + near * x_ref[1]
    pre_ref[0] = jnp.where(upper, x_ref[0], 0.0)
    pre_ref[1] = jnp.where(upper, 0.0, x_ref[1])


def quad_kernel(tot_ref, x_ref, pre_ref, send_ref, pre2_ref):
    e = lax.axis_index("gz")
    upper = ((e // 2) % 2) == 1
    odd = (e % 2) == 1
    two = STEP_Z * STEP_Z
    near, far = jnp.where(upper, 1.0, two), jnp.where(upper, two, 1.0)
    top = (e // 4) == 1
    send_ref[...] = jnp.where(top, far * tot_ref[1] + near * x_ref[1], near * tot_ref[0] + far * x_ref[0])
    low = jnp.where(odd, STEP_Z, 1.0)
    high = jnp.where(odd, 1.0, STEP_Z)
    pre2_ref[0] = pre_ref[0] + jnp.where(upper, low * x_ref[0], 0.0)
    pre2_ref[1] = pre_ref[1] + jnp.where(upper, 0.0, high * x_ref[1])


def own_kernel(p0_ref, p1_ref, p2_ref, p3_ref, tz_ref, dz_ref, p4):
    x = lax.rem(lax.axis_index("gy"), GX)
    for i, ref in enumerate((p0_ref, p1_ref, p2_ref, p3_ref)):
        p4[lax.bitwise_xor(x, i)] = ref[...]
    own = weights(tz_ref, 0)
    for k in range(2):
        for t in range(16):
            p = p4[t // 4, k, :, (t % 4) * 128 : (t % 4 + 1) * 128]
            dz_ref[k, :, t * 128 : (t + 1) * 128] = weighted(own, p)


def near_kernel(loc_ref, dz_ref, tv_ref, o_ref):
    for l in range(LY):
        for t in range(NX // 128):
            cols = slice(t * 128, (t + 1) * 128)
            o_ref[l, :, cols] = (loc_ref[l, :, cols] + tv_ref[l : l + 1, :] * dz_ref[0, :, cols]
                                 + tv_ref[16 + l : 17 + l, :] * dz_ref[1, :, cols])


def final_kernel(near_ref, pre_ref, x_ref, r_ref, tz_ref, tv_ref, o_hbm, cl, ch, o_ref, sems):
    e = lax.axis_index("gz")
    low_rows, high_rows = [], []
    for q in range(GX):
        lo = jnp.zeros((8, 128), F32)
        hi = jnp.zeros((8, 128), F32)
        for p in range(DZ):
            part = r_ref[q * DZ + p]
            lo += jnp.where(p < e, part, 0.0)
            hi += jnp.where(p > e, part, 0.0)
        low_rows.append(lo)
        high_rows.append(hi)
    top = (e // 4) == 1
    at = lax.rem(e, 4)
    power = lambda k: jnp.where(k == 0, 1.0, jnp.where(k == 1, STEP_Z, jnp.where(k == 2, STEP_Z**2, STEP_Z**3)))
    up = jnp.where(top, power(at), 0.0)
    down = jnp.where(top, 0.0, power(3 - at))
    ga, gb = tv_ref[0:16], tv_ref[16:32]
    for t in range(NX // 128):
        cols = slice(t * 128, (t + 1) * 128)
        q, i = t // 4, t % 4
        lo, hi = low_rows[q], high_rows[q]
        cl[:, cols] = (pre_ref[0, :, cols] + up * x_ref[:, cols]) + (ga * lo[i : i + 1] + gb * lo[4 + i : 5 + i])
        ch[:, cols] = (pre_ref[1, :, cols] + down * x_ref[:, cols]) + (ga * hi[i : i + 1] + gb * hi[4 + i : 5 + i])
    hl, hh = tz_ref[16:24], tz_ref[24:32]
    stores = []
    for l in range(LY):
        for t in range(NX // 128):
            cols = slice(t * 128, (t + 1) * 128)
            o_ref[l, :, cols] = near_ref[l, :, cols] + (hl * cl[l : l + 1, cols] + hh * ch[l : l + 1, cols])
        if l % 4 == 3:
            i = l // 4
            stores += start((o_ref.at[pl.ds(l - 3, 4)], o_hbm.at[pl.ds(l - 3, 4)], sems.at[i]))
    for store in stores:
        store.wait()


VMEM = pl.BlockSpec(memory_space=pltpu.VMEM)
HBM = pl.BlockSpec(memory_space=pltpu.HBM)
FULL, QUARTER, SUMS_Z = (LY, LZ, NX), (2, LZ, Q), (2, LY, NX)


def call(kernel, outs, ins, out_specs, scratch, mib, name, cost=None):
    if cost is not None:
        cost = pl.CostEstimate(flops=cost[0], bytes_accessed=cost[1], transcendentals=0)
    return pl.pallas_call(
        kernel,
        out_shape=tuple(o if isinstance(o, jax.ShapeDtypeStruct) else jax.ShapeDtypeStruct(o, F32) for o in outs),
        in_specs=ins,
        out_specs=tuple(out_specs),
        scratch_shapes=scratch,
        compiler_params=pltpu.CompilerParams(vmem_limit_bytes=mib * 2**20),
        cost_estimate=cost,
        name=name,
    )


def pairs(count, odd):
    out = []
    for i in range(count):
        j = i + 1 if (i % 2 == 1) == odd else i - 1
        if 0 <= j < count:
            out.append((i, j))
    return out


def across(value, axis, count, bit):
    return lax.ppermute(value, axis, [(i, i ^ bit) for i in range(count)])


tie = lambda *values: lax.optimization_barrier(values)
SMALL = (10**5, 5 * 10**5)
LAYER = [[(z * GX + x) * DZ + e for x in range(GX) for e in range(DZ)] for z in range(GZ)]
COLUMN = [[z * GX + x for z in range(GZ)] for x in range(GX)]


def on_device(temp, vel):
    dma = pltpu.SemaphoreType.DMA
    bf = lambda *shape: jax.ShapeDtypeStruct(shape, BF16)
    y1, y2, z1, z2 = call(
        faces_kernel, [(LZ, NX), (LZ, NX), (LY, NX), (LY, NX)], [HBM], [VMEM] * 4, [pltpu.VMEM(FULL, F32), dma((LY // 4,))], 62, "faces"
    )(temp)
    y1 = lax.ppermute(y1, "gy", pairs(DY, False))
    y2 = lax.ppermute(y2, "gy", pairs(DY, True))
    z1 = lax.ppermute(z1, "gz", pairs(DZ, False))
    z2 = lax.ppermute(z2, "gz", pairs(DZ, True))
    f, mf, ml, wx, tv, tz = call(
        inner_kernel,
        [FULL, bf(ROWS + 32, 256), bf(ROWS + 32, 128), bf(2, XB, XB), (128, 128), (32, 128)],
        [VMEM] * 2,
        [VMEM] * 6,
        [],
        16,
        "inner",
        (10**7, 8 * 10**6),
    )(temp, vel)
    f, *mine = call(
        source_kernel,
        [FULL] + [QUARTER] * 4,
        [VMEM] * 8,
        [VMEM] * 5,
        [
            pltpu.VMEM((NB, 16, XB), BF16),
            pltpu.VMEM((NB, 16, XB), BF16),
            pltpu.VMEM((NB, 16, XB), F32),
            pltpu.VMEM((GX, 2, LZ, Q), F32),
        ],
        16,
        "source",
    )(f, vel, y1, y2, z1, z2, wx, tv)
    sets = [mine[0]] + [across(mine[i], "gy", DY, i) for i in (1, 2, 3)]
    loc, c = call(
        local_kernel,
        [FULL, SUMS_Z],
        [VMEM] * 4,
        [VMEM] * 2,
        [
            pltpu.VMEM((NB, ROWS, XB), BF16),
            pltpu.VMEM((NB, ROWS, XB), BF16),
            pltpu.VMEM((NB, ROWS, XB), F32),
            pltpu.VMEM((2 * ROWS, NX), BF16),
        ],
        16,
        "local",
        (2 * 10**9, 8 * 10**6),
    )(f, wx, mf, ml)
    c, sets[1] = tie(c, sets[1])
    x1 = across(c, "gz", DZ, 1)
    tots = call(group_kernel, [(GZ, LZ, Q)], [VMEM] * 5, [VMEM], [], 4, "group", SMALL)(*sets, tv)[0]
    r1 = lax.all_to_all(tots, "gy", 0, 0, axis_index_groups=COLUMN)
    tot, pre = call(pair_kernel, [SUMS_Z] * 2, [VMEM] * 2, [VMEM] * 2, [], 4, "pair", SMALL)(c, x1)
    x2 = across(tot, "gz", DZ, 2)
    r1, tot, pre = tie(r1, tot, pre)
    *mine, s = call(
        spread_kernel, [QUARTER] * 4 + [(GX, 64, 128)], [VMEM] * 7, [VMEM] * 5, [], 4, "spread", SMALL
    )(*sets, r1, tv, tz)
    r3 = lax.all_to_all(s.reshape(GX * DZ, 8, 128), ("gy", "gz"), 0, 0, axis_index_groups=LAYER)
    sets = [mine[0]] + [across(mine[i], "gy", DY, i) for i in (1, 2, 3)]
    x2, sets[0] = tie(x2, sets[0])
    send, pre = call(quad_kernel, [(LY, NX), SUMS_Z], [VMEM] * 3, [VMEM] * 2, [], 4, "quad", SMALL)(tot, x2, pre)
    x3 = across(send, "gz", DZ, 4)
    dz = call(
        own_kernel, [(2, LZ, NX)], [VMEM] * 5, [VMEM], [pltpu.VMEM((GX, 2, LZ, Q), F32)], 8, "own", SMALL
    )(*sets, tz)[0]
    near = call(near_kernel, [FULL], [VMEM] * 3, [VMEM], [], 8, "near", (10**6, 2 * 10**6))(loc, dz, tv)[0]
    return call(
        final_kernel,
        [FULL],
        [VMEM] * 6,
        [HBM],
        [pltpu.VMEM((LY, NX), F32), pltpu.VMEM((LY, NX), F32), pltpu.VMEM(FULL, F32), dma((4,))],
        16,
        "final",
    )(near, pre, x3, r3, tz, tv)[0]


def solution(mesh):
    return jax.shard_map(
        on_device,
        mesh=mesh,
        in_specs=(P("gy", "gz", None), P(None, "gy", "gz", None)),
        out_specs=P("gy", "gz", None),
        check_vma=False,
    )
```
